128 devices in a mesh: gx: 8 (over y_lo, z), gy: 16 (over x, y_hi, core).
Axes of the slice: x: 4, y: 4 (y_hi: 2, y_lo: 2; y = y_hi * 2 + y_lo), z: 4, core: 2. Of those that a mesh axis runs over, the one named last changes fastest.
Arguments:
- matrix: float32 [262144, 512], P(('gx', 'gy'))
- sign_flips: int32 [262144], P(('gx', 'gy')), may hold values from -1 to 1, as said below
- sampled_rows: int32 [32768], P(('gx', 'gy')), may hold values from 0 to 2047, as said below
Outputs:
- gram: float32 [512, 512], P(('gx', 'gy'))
The draws below stay inside these ranges and needn't reach their ends.
Inputs may be any that keep to these rules, and one draw needn't show every extreme that they name: `sign_flips`: each entry is -1 or +1. `sampled_rows`: within each aligned block of 256 entries the offsets are distinct and ascending; block b refers to rows b * 2048 onward.
All inputs are finite; a program needn't handle non-finite values.
Results may differ from the reference program's by a relative error of at most 0.00005.
Values sent between devices are 32-bit elements; how exact they have to be, the bound alone decides.
No kernel may reach another device: no remote copies, remote signals or barrier semaphores. Data moves between devices by JAX's collectives and lax.ppermute only.
A program may use at most 64 MiB of HBM per device.

```python
import math
import jax
import jax.numpy as jnp
from jax import lax

D = 512
ROWS_DEV = 2048
SAMP_DEV = 256
N_GX = 8
N_GY = 16


def draw_matrix(key, part):
    key = jax.random.fold_in(key, 11)
    keys = jax.random.split(key, 5)
    total_rows = ROWS_DEV * N_GX * N_GY
    base = jax.random.normal(keys[0], (total_rows, D), jnp.float32)
    common_weight = 0.7
    common = jax.random.normal(keys[1], (total_rows, 1), jnp.float32)
    mixing = jax.random.uniform(keys[2], (1, D), jnp.float32, -1.0, 1.0)
    base = base + common_weight * common * mixing
    row_scale = 0.3 * jnp.exp(jax.random.uniform(keys[3], (total_rows, 1), jnp.float32, 0.0, math.log(10.0)))
    col_scale = 0.3 * jnp.exp(jax.random.uniform(keys[4], (1, D), jnp.float32, 0.0, math.log(10.0)))
    return (base * row_scale * col_scale).astype(jnp.float32)


def draw_sign_flips(key, part):
    key = jax.random.fold_in(key, 23)
    total_rows = ROWS_DEV * N_GX * N_GY
    return (2 * jax.random.randint(key, (total_rows,), 0, 2) - 1).astype(jnp.int32)


def draw_sampled_rows(key, part):
    key = jax.random.fold_in(key, 37)
    device_count = N_GX * N_GY
    keys = jax.random.split(key, device_count)

    def one_block(block_key):
        inner = jax.random.permutation(block_key, ROWS_DEV - 2)[:SAMP_DEV - 2] + 1
        ends = jnp.array([0, ROWS_DEV - 1], dtype=jnp.int32)
        return jnp.concatenate([ends, inner.astype(jnp.int32)])
    chosen = jax.vmap(one_block)(keys)
    return jnp.sort(chosen, axis=1).reshape(-1).astype(jnp.int32)


def setup_inputs(seed: int = 0) -> dict:
    key_list = jax.random.split(jax.random.key(seed), 4)
    matrix = draw_matrix(jax.random.fold_in(key_list[3], 71), 0)
    sign_flips = draw_sign_flips(jax.random.fold_in(key_list[3], 71), 0)
    sampled_rows = draw_sampled_rows(jax.random.fold_in(key_list[3], 71), 0)
    return {"matrix": matrix, "sign_flips": sign_flips, "sampled_rows": sampled_rows}


def reference(matrix, sign_flips, sampled_rows):
    row_total = matrix.shape[0]
    col_count = matrix.shape[1]
    current = matrix * sign_flips.astype(jnp.float32)[:, None]
    stride = 1
    while stride < row_total:
        shaped = current.reshape(row_total // (2 * stride), 2, stride, col_count)
        upper_half = shaped[:, 0]
        lower_half = shaped[:, 1]
        current = jnp.stack([upper_half + lower_half, upper_half - lower_half], axis=1).reshape(row_total, col_count)
        stride = stride * 2
    transformed = current * (1.0 / math.sqrt(row_total))
    device_count = N_GX * N_GY
    offsets = (jnp.arange(device_count, dtype=jnp.int32) * ROWS_DEV)[:, None]
    global_rows = (sampled_rows.reshape(device_count, -1) + offsets).reshape(-1).astype(jnp.int32)
    picked = jnp.take(transformed, global_rows, axis=0)
    product = lax.dot_general(picked, picked, (((0,), (0,)), ((), ())), precision=lax.Precision.HIGHEST, preferred_element_type=jnp.float32)
    return product * (1.0 / global_rows.shape[0])
```

```python
import jax
import jax.numpy as jnp
import numpy as np
from jax import lax
from jax.experimental import pallas as pl
from jax.experimental.pallas import tpu as pltpu
from jax.sharding import Mesh, PartitionSpec as P

AXES = ("yl", "z", "x", "yh", "c")
CHIPS = ("yl", "z", "x", "yh")
TILE = 256
LANES = 128


def hadamard(order):
    grid = np.arange(order)[:, None] & np.arange(order)[None, :]
    parity = np.zeros((order, order), np.int32)
    for bit in range(order.bit_length() - 1):
        parity ^= (grid >> bit) & 1
    return 1.0 - 2.0 * parity


def butterfly(value):
    count = value.shape[0]
    if count == 1:
        return value
    half = count // 2
    first, second = value[:half], value[half:]
    return jnp.concatenate([butterfly(first + second), butterfly(first - second)])


def split2(value):
    high = value.astype(jnp.bfloat16)
    low = (value - high.astype(jnp.float32)).astype(jnp.bfloat16)
    return high, low


def split3(value):
    high = value.astype(jnp.bfloat16)
    rest = value - high.astype(jnp.float32)
    middle = rest.astype(jnp.bfloat16)
    low = (rest - middle.astype(jnp.float32)).astype(jnp.bfloat16)
    return high, middle, low


def mix_kernel(signs, table, block, mixed):
    groups = signs.shape[0]
    width = block.shape[1]
    for group in range(groups):
        rows = pl.ds(group * TILE, TILE)
        left = (table[...] * signs[group : group + 1, :]).astype(jnp.bfloat16)
        high, middle, low = split3(block[rows, :])
        mixed[rows, :] = (
            jnp.dot(left, low, preferred_element_type=jnp.float32)
            + jnp.dot(left, middle, preferred_element_type=jnp.float32)
            + jnp.dot(left, high, preferred_element_type=jnp.float32)
        )
    for start in range(0, TILE, 8):
        for lane in range(0, width, LANES):
            value = jnp.stack(
                [mixed[group * TILE + start : group * TILE + start + 8, lane : lane + LANES] for group in range(groups)]
            )
            value = butterfly(value)
            for group in range(groups):
                mixed[group * TILE + start : group * TILE + start + 8, lane : lane + LANES] = value[group]


def local_mix(matrix, signs):
    rows, columns = matrix.shape
    groups = rows // TILE
    width = 256
    return pl.pallas_call(
        mix_kernel,
        grid=(columns // width,),
        out_shape=jax.ShapeDtypeStruct((rows, columns), jnp.float32),
        in_specs=[
            pl.BlockSpec((groups, TILE), lambda i: (0, 0)),
            pl.BlockSpec((TILE, TILE), lambda i: (0, 0)),
            pl.BlockSpec((rows, width), lambda i: (0, i)),
        ],
        out_specs=pl.BlockSpec((rows, width), lambda i: (0, i)),
        compiler_params=pltpu.CompilerParams(vmem_limit_bytes=48 << 20),
        cost_estimate=pl.CostEstimate(flops=2 * rows * TILE * columns * 3, bytes_accessed=8 * rows * columns, transcendentals=0),
        name="local_mix",
    )(signs.reshape(groups, TILE).astype(jnp.float32), jnp.asarray(hadamard(TILE), jnp.float32), matrix)


def gram_kernel(scale, block, chosen, gram, work, parts):
    devices, inner, columns = block.shape
    near = 8
    far = devices // near
    for lane in range(0, columns, LANES):
        lanes = pl.ds(lane, LANES)
        for tile in range(0, inner, 8):
            sub = pl.ds(tile, 8)
            for start in range(near):
                value = jnp.stack([block[start + near * step, sub, lanes] for step in range(far)])
                value = butterfly(value)
                for step in range(far):
                    work[start + near * step] = value[step]
            for step in range(far):
                value = butterfly(work[near * step : near * (step + 1)])
                value = value * chosen[near * step : near * (step + 1), sub, :]
                value = value.reshape(near * 8, LANES)
                high, low = split2(value)
                base = (tile // 8 * devices + near * step) * 8
                parts[pl.ds(base, near * 8), lanes] = high
                parts[pl.ds(base, near * 8), pl.ds(columns + lane, LANES)] = low
    product = lax.dot_general(
        parts[:, :columns], parts[...], (((0,), (0,)), ((), ())), preferred_element_type=jnp.float32
    )
    cross = product[:, columns:]
    gram[...] = (product[:, :columns] + (cross + cross.T)) * scale


def local_gram(block, chosen, scale):
    devices, inner, columns = block.shape
    whole = lambda *shape: pl.BlockSpec(shape, lambda: (0,) * len(shape))
    rows = devices * inner
    return pl.pallas_call(
        lambda *refs: gram_kernel(scale, *refs),
        out_shape=jax.ShapeDtypeStruct((columns, columns), jnp.float32),
        in_specs=[whole(devices, inner, columns), whole(devices, inner, LANES)],
        out_specs=whole(columns, columns),
        scratch_shapes=[
            pltpu.VMEM((devices, 8, LANES), jnp.float32),
            pltpu.VMEM((rows, 2 * columns), jnp.bfloat16),
        ],
        compiler_params=pltpu.CompilerParams(vmem_limit_bytes=48 << 20),
        cost_estimate=pl.CostEstimate(flops=4 * rows * columns * columns, bytes_accessed=4 * rows * columns, transcendentals=0),
        name="local_gram",
    )(block, chosen)


def swap_core(value):
    return lax.ppermute(value, "c", [(0, 1), (1, 0)])


def local(matrix, sign_flips, sampled_rows):
    rows, columns = matrix.shape
    devices = lax.axis_size(AXES)
    chips = devices // 2
    inner = rows // devices
    samples = sampled_rows.shape[0] * devices
    scale = 1.0 / (rows * devices) / samples

    mixed = local_mix(matrix, sign_flips)
    hits = sampled_rows[None, :] == lax.iota(jnp.int32, rows)[:, None]
    flags = jnp.max(hits.astype(jnp.float32), axis=1).reshape(devices, inner)
    blocks = lax.all_to_all(mixed, AXES, 0, 0, tiled=True)
    flags = lax.all_to_all(flags, AXES, 0, 0, tiled=True)
    chosen = jnp.broadcast_to(flags[:, :, None], (devices, inner, LANES))
    partial = local_gram(blocks.reshape(devices, inner, columns), chosen, scale)

    core = lax.axis_index("c")
    out_rows = columns // devices
    halves = partial.reshape(chips, 2, out_rows, columns)
    mine = lax.dynamic_index_in_dim(halves, core, 1, keepdims=False)
    other = lax.dynamic_index_in_dim(halves, 1 - core, 1, keepdims=False)
    summed = mine + swap_core(other)
    pieces = lax.all_to_all(summed, CHIPS, 0, 0, tiled=True)
    return jnp.sum(pieces, axis=0)


def solution(mesh):
    fine = Mesh(mesh.devices.reshape(2, 4, 4, 2, 2), AXES)
    return jax.shard_map(
        local, mesh=fine, in_specs=(P(AXES, None), P(AXES), P(AXES)), out_specs=P(AXES, None), check_vma=False
    )
```

```python
import jax
import jax.numpy as jnp
from jax import lax
from jax.experimental import pallas as pl
from jax.experimental.pallas import tpu as pltpu
from jax.sharding import Mesh, PartitionSpec as P

AXES = ("yl", "z", "x", "yh", "c")
CHIPS = ("yl", "z", "x", "yh")
TILE = 256
LANES = 128
SUBLANES = 8
VMEM_BYTES = 32 << 20


def butterfly(value):
    count = value.shape[0]
    if count == 1:
        return value
    half = count // 2
    first, second = value[:half], value[half:]
    return jnp.concatenate([butterfly(first + second), butterfly(first - second)])


def split2(value):
    high = value.astype(jnp.bfloat16)
    low = (value - high.astype(jnp.float32)).astype(jnp.bfloat16)
    return high, low


def split3(value):
    high = value.astype(jnp.bfloat16)
    rest = value - high.astype(jnp.float32)
    middle = rest.astype(jnp.bfloat16)
    low = (rest - middle.astype(jnp.float32)).astype(jnp.bfloat16)
    return high, middle, low


def sign_table():
    row = lax.broadcasted_iota(jnp.int32, (TILE, TILE), 0)
    column = lax.broadcasted_iota(jnp.int32, (TILE, TILE), 1)
    shared = row & column
    shared = shared ^ (shared >> 4)
    shared = shared ^ (shared >> 2)
    shared = shared ^ (shared >> 1)
    return (1 - 2 * (shared & 1)).astype(jnp.float32)


def flag_lines(offsets, devices, inner):
    count = offsets.shape[1]
    place = lax.broadcasted_iota(jnp.int32, (devices, count), 0)
    left = jnp.where(place == offsets // inner, 1.0, 0.0)
    lane = lax.broadcasted_iota(jnp.int32, (LANES, count), 0)
    right = jnp.where(lane == offsets % inner, 1.0, 0.0)
    return lax.dot_general(
        left.astype(jnp.bfloat16),
        right.astype(jnp.bfloat16),
        (((1,), (1,)), ((), ())),
        preferred_element_type=jnp.float32,
    )


def mix_kernel(devices, signs_far, sampled_far, block, mixed, held, signs, sampled, arrive, small):
    groups, _, columns = block.shape
    inner = groups * TILE // devices
    lines = mixed.shape[0] // devices
    lane_tiles = TILE // LANES
    column_tiles = columns // LANES
    signs_copy = pltpu.make_async_copy(signs_far, signs, small.at[0])
    sampled_copy = pltpu.make_async_copy(sampled_far, sampled, small.at[1])
    incoming = [pltpu.make_async_copy(block.at[g], held.at[g], arrive.at[g]) for g in range(groups)]
    for copy in [signs_copy, sampled_copy] + incoming:
        copy.start()
    table = sign_table()
    signs_copy.wait()
    sampled_copy.wait()
    flips = signs[...].astype(jnp.float32)
    offsets = jnp.concatenate([sampled[i : i + 1, :] for i in range(sampled.shape[0])], axis=1)
    flags = flag_lines(offsets, devices, inner)
    for number in range(devices):
        mixed[pl.ds(number * lines + lines - 1, 1), :] = flags[number : number + 1, :]
    for g in range(groups):
        left = jnp.concatenate(
            [
                table[:, t * LANES : (t + 1) * LANES] * flips[g * lane_tiles + t : g * lane_tiles + t + 1, :]
                for t in range(lane_tiles)
            ],
            axis=1,
        ).astype(jnp.bfloat16)
        incoming[g].wait()
        high, middle, low = split3(held[g])
        held[g] = (
            jnp.dot(left, low, preferred_element_type=jnp.float32)
            + jnp.dot(left, middle, preferred_element_type=jnp.float32)
            + jnp.dot(left, high, preferred_element_type=jnp.float32)
        )
    for start in range(0, TILE, SUBLANES):
        for column in range(column_tiles):
            value = butterfly(held[:, pl.ds(start, SUBLANES), pl.ds(column * LANES, LANES)])
            tile = (start % inner) // SUBLANES * column_tiles + column
            for g in range(groups):
                first = (g * TILE + start) // inner * lines + tile * SUBLANES
                mixed[pl.ds(first, SUBLANES), :] = value[g]


def local_mix(matrix, signs, sampled, devices):
    rows, columns = matrix.shape
    groups = rows // TILE
    lines = rows // devices * columns // LANES + 1
    far = pl.BlockSpec(memory_space=pltpu.HBM)
    stay = lambda value: pltpu.with_memory_space_constraint(value, pltpu.HBM)
    return pl.pallas_call(
        lambda *refs: mix_kernel(devices, *refs),
        out_shape=pltpu.VMEM((devices * lines, LANES), jnp.float32),
        in_specs=[far, far, far],
        out_specs=pl.BlockSpec(memory_space=pltpu.VMEM),
        scratch_shapes=[
            pltpu.VMEM((groups, TILE, columns), jnp.float32),
            pltpu.VMEM((rows // LANES, LANES), jnp.int32),
            pltpu.VMEM((sampled.shape[0] // LANES, LANES), jnp.int32),
            pltpu.SemaphoreType.DMA((groups,)),
            pltpu.SemaphoreType.DMA((2,)),
        ],
        compiler_params=pltpu.CompilerParams(vmem_limit_bytes=VMEM_BYTES),
        cost_estimate=pl.CostEstimate(
            flops=6 * rows * TILE * columns, bytes_accessed=8 * rows * columns, transcendentals=0
        ),
        name="local_mix",
    )(
        stay(signs.reshape(-1, LANES)),
        stay(sampled.reshape(-1, LANES)),
        stay(matrix.reshape(groups, TILE, columns)),
    )


def gram_kernel(scale, devices, core, block, mine, other, chosen, work, parts):
    lines = block.shape[0] // devices
    columns = mine.shape[1]
    column_tiles = columns // LANES
    tiles = lines // SUBLANES // column_tiles
    near = SUBLANES
    far = devices // near
    sublane = lax.broadcasted_iota(jnp.int32, (SUBLANES, LANES), 0)
    lane = lax.broadcasted_iota(jnp.int32, (SUBLANES, LANES), 1)
    spread = [
        jnp.broadcast_to(block[pl.ds(number * lines + lines - 1, 1), :], (SUBLANES, LANES))
        for number in range(devices)
    ]
    ones = jnp.ones((LANES, LANES), jnp.bfloat16)
    for tile in range(tiles):
        own = lane == sublane + tile * SUBLANES
        flags = jnp.concatenate([jnp.where(own, value, 0.0) for value in spread]).astype(jnp.bfloat16)
        chosen[tile] = jnp.dot(flags, ones, preferred_element_type=jnp.float32).reshape(devices, SUBLANES, LANES)
    product = None
    for tile in range(tiles):
        for column in range(column_tiles):
            number = tile * column_tiles + column
            lanes = pl.ds(column * LANES, LANES)
            slot = work.at[number % 2]
            for start in range(near):
                value = butterfly(
                    jnp.stack(
                        [
                            block[pl.ds((start + near * step) * lines + number * SUBLANES, SUBLANES), :]
                            for step in range(far)
                        ]
                    )
                )
                for step in range(far):
                    slot[start + near * step] = value[step]
            for step in range(far):
                group = pl.ds(near * step, near)
                value = butterfly(slot[group]) * chosen[tile, group]
                high, low = split2(value.reshape(near * SUBLANES, LANES))
                rows = pl.ds(near * SUBLANES * step, near * SUBLANES)
                parts[tile, rows, lanes] = high
                parts[tile, rows, pl.ds(columns + column * LANES, LANES)] = low
        term = lax.dot_general(
            parts[tile, :, :columns], parts[tile], (((0,), (0,)), ((), ())), preferred_element_type=jnp.float32
        )
        product = term if product is None else product + term
    cross = product[:, columns:]
    gram = (product[:, :columns] + (cross + cross.T)) * scale
    pairs = gram.reshape(columns // 16, 2, 8, columns)
    first, second = pairs[:, 0], pairs[:, 1]
    upper = lax.broadcasted_iota(jnp.int32, first.shape, 1) < 4
    flat = lambda value: value.reshape(columns // 2, columns)
    turn = lambda value: pltpu.roll(value, 4, 1)
    zero = flat(jnp.where(upper, first, turn(second)))
    one = flat(jnp.where(upper, turn(first), second))
    here = core[0] == 0
    mine[...] = jnp.where(here, zero, one)
    other[...] = jnp.where(here, one, zero)


def local_gram(block, core, devices, columns, scale):
    lines = block.shape[0] // devices
    tiles = lines * LANES // columns // SUBLANES
    half = jax.ShapeDtypeStruct((columns // 2, columns), jnp.float32)
    vmem = pl.BlockSpec(memory_space=pltpu.VMEM)
    return pl.pallas_call(
        lambda *refs: gram_kernel(scale, devices, *refs),
        out_shape=(half, half),
        in_specs=[pl.BlockSpec(memory_space=pltpu.SMEM), vmem],
        out_specs=(vmem, vmem),
        scratch_shapes=[
            pltpu.VMEM((tiles, devices, SUBLANES, LANES), jnp.float32),
            pltpu.VMEM((2, devices, SUBLANES, LANES), jnp.float32),
            pltpu.VMEM((tiles, devices * SUBLANES, 2 * columns), jnp.bfloat16),
        ],
        compiler_params=pltpu.CompilerParams(vmem_limit_bytes=VMEM_BYTES),
        cost_estimate=pl.CostEstimate(
            flops=4 * tiles * SUBLANES * devices * columns * columns,
            bytes_accessed=4 * devices * lines * LANES,
            transcendentals=0,
        ),
        name="local_gram",
    )(core.reshape(1), block)


def local(matrix, sign_flips, sampled_rows):
    rows, columns = matrix.shape
    devices = lax.axis_size(AXES)
    chips = devices // 2
    samples = sampled_rows.shape[0] * devices
    scale = 1.0 / (rows * devices) / samples

    core = lax.axis_index("c")
    mixed = local_mix(matrix, sign_flips, sampled_rows, devices)
    mixed, core = lax.optimization_barrier((mixed, core))
    lines = mixed.shape[0] // devices
    blocks = lax.all_to_all(mixed.reshape(devices, lines * LANES), AXES, 0, 0, tiled=True)
    mine, other = local_gram(blocks.reshape(devices * lines, LANES), core, devices, columns, scale)

    summed = mine + lax.ppermute(other, "c", [(0, 1), (1, 0)])
    pieces = lax.all_to_all(summed.reshape(chips, -1, columns), CHIPS, 0, 0, tiled=True)
    return jnp.sum(pieces, axis=0)


def solution(mesh):
    fine = Mesh(mesh.devices.reshape(2, 4, 4, 2, 2), AXES)
    return jax.shard_map(
        local, mesh=fine, in_specs=(P(AXES, None), P(AXES), P(AXES)), out_specs=P(AXES, None), check_vma=False
    )
```

```python
import jax
import jax.numpy as jnp
from jax import lax
from jax.experimental import pallas as pl
from jax.experimental.pallas import tpu as pltpu
from jax.sharding import Mesh, PartitionSpec as P

AXES = ("yl", "z", "x", "yh", "c")
CHIPS = ("yl", "z", "x", "yh")
TILE = 128
LANES = 128
SUBLANES = 8
VMEM_BYTES = 32 << 20


def butterfly(value):
    count = value.shape[0]
    if count == 1:
        return value
    half = count // 2
    first, second = value[:half], value[half:]
    return jnp.concatenate([butterfly(first + second), butterfly(first - second)])


def split2(value):
    high = value.astype(jnp.bfloat16)
    low = (value - high.astype(jnp.float32)).astype(jnp.bfloat16)
    return high, low


def split3(value):
    high = value.astype(jnp.bfloat16)
    rest = value - high.astype(jnp.float32)
    middle = rest.astype(jnp.bfloat16)
    low = (rest - middle.astype(jnp.float32)).astype(jnp.bfloat16)
    return high, middle, low


def sign_table():
    row = lax.broadcasted_iota(jnp.int32, (TILE, TILE), 0)
    column = lax.broadcasted_iota(jnp.int32, (TILE, TILE), 1)
    shared = row & column
    shared = shared ^ (shared >> 4)
    shared = shared ^ (shared >> 2)
    shared = shared ^ (shared >> 1)
    return (1 - 2 * (shared & 1)).astype(jnp.float32)


def flag_lines(offsets, devices, inner):
    count = offsets.shape[1]
    place = lax.broadcasted_iota(jnp.int32, (devices, count), 0)
    left = jnp.where(place == offsets // inner, 1.0, 0.0)
    lane = lax.broadcasted_iota(jnp.int32, (LANES, count), 0)
    right = jnp.where(lane == offsets % inner, 1.0, 0.0)
    return lax.dot_general(
        left.astype(jnp.bfloat16),
        right.astype(jnp.bfloat16),
        (((1,), (1,)), ((), ())),
        preferred_element_type=jnp.float32,
    )


def mix_kernel(devices, signs_far, sampled_far, block, mixed, held, signs, sampled, arrive, small):
    groups, _, columns = block.shape
    inner = groups * TILE // devices
    lines = mixed.shape[0] // devices
    column_tiles = columns // LANES
    quarter = groups // arrive.shape[0]
    signs_copy = pltpu.make_async_copy(signs_far, signs, small.at[0])
    sampled_copy = pltpu.make_async_copy(sampled_far, sampled, small.at[1])
    incoming = [
        pltpu.make_async_copy(block.at[pl.ds(start, quarter)], held.at[pl.ds(start, quarter)], arrive.at[number])
        for number, start in enumerate(range(0, groups, quarter))
    ]
    for copy in [signs_copy, sampled_copy] + incoming:
        copy.start()
    table = sign_table()
    signs_copy.wait()
    flips = signs[...].astype(jnp.float32)
    due = {0: incoming[:1], quarter: incoming[1:-1], groups - quarter: incoming[-1:]}
    for g in range(groups):
        for copy in due.get(g, []):
            copy.wait()
        left = (table * flips[g : g + 1, :]).astype(jnp.bfloat16)
        high, middle, low = split3(held[g])
        held[g] = jnp.dot(left, low, preferred_element_type=jnp.float32) + jnp.dot(
            jnp.concatenate([left, left], axis=1),
            jnp.concatenate([middle, high], axis=0),
            preferred_element_type=jnp.float32,
        )
    sampled_copy.wait()
    offsets = jnp.concatenate([sampled[i : i + 1, :] for i in range(sampled.shape[0])], axis=1)
    flags = flag_lines(offsets, devices, inner)
    for number in range(devices):
        mixed[pl.ds(number * lines + lines - 1, 1), :] = flags[number : number + 1, :]
    for start in range(0, TILE, SUBLANES):
        for column in range(column_tiles):
            value = butterfly(held[:, pl.ds(start, SUBLANES), pl.ds(column * LANES, LANES)])
            tile = (start % inner) // SUBLANES * column_tiles + column
            for g in range(groups):
                first = (g * TILE + start) // inner * lines + tile * SUBLANES
                mixed[pl.ds(first, SUBLANES), :] = value[g]


def local_mix(matrix, signs, sampled, devices):
    rows, columns = matrix.shape
    groups = rows // TILE
    lines = rows // devices * columns // LANES + 1
    far = pl.BlockSpec(memory_space=pltpu.HBM)
    stay = lambda value: pltpu.with_memory_space_constraint(value, pltpu.HBM)
    return pl.pallas_call(
        lambda *refs: mix_kernel(devices, *refs),
        out_shape=pltpu.VMEM((devices * lines, LANES), jnp.float32),
        in_specs=[far, far, far],
        out_specs=pl.BlockSpec(memory_space=pltpu.VMEM),
        scratch_shapes=[
            pltpu.VMEM((groups, TILE, columns), jnp.float32),
            pltpu.VMEM((rows // LANES, LANES), jnp.int32),
            pltpu.VMEM((sampled.shape[0] // LANES, LANES), jnp.int32),
            pltpu.SemaphoreType.DMA((4,)),
            pltpu.SemaphoreType.DMA((2,)),
        ],
        compiler_params=pltpu.CompilerParams(vmem_limit_bytes=VMEM_BYTES),
        cost_estimate=pl.CostEstimate(
            flops=6 * rows * TILE * columns, bytes_accessed=8 * rows * columns, transcendentals=0
        ),
        name="local_mix",
    )(
        stay(signs.reshape(-1, LANES)),
        stay(sampled.reshape(-1, LANES)),
        stay(matrix.reshape(groups, TILE, columns)),
    )


def gram_kernel(scale, devices, core, block, mine, other, chosen, work, parts):
    lines = block.shape[0] // devices
    columns = mine.shape[1]
    column_tiles = columns // LANES
    tiles = lines // SUBLANES // column_tiles
    near = SUBLANES
    far = devices // near
    sublane = lax.broadcasted_iota(jnp.int32, (SUBLANES, LANES), 0)
    lane = lax.broadcasted_iota(jnp.int32, (SUBLANES, LANES), 1)
    spread = [
        jnp.broadcast_to(block[pl.ds(number * lines + lines - 1, 1), :], (SUBLANES, LANES))
        for number in range(devices)
    ]
    ones = jnp.ones((LANES, LANES), jnp.bfloat16)
    for tile in range(tiles):
        own = lane == sublane + tile * SUBLANES
        flags = jnp.concatenate([jnp.where(own, value, 0.0) for value in spread]).astype(jnp.bfloat16)
        chosen[tile] = jnp.dot(flags, ones, preferred_element_type=jnp.float32).reshape(devices, SUBLANES, LANES)
    depth = devices * SUBLANES
    for tile in range(tiles):
        for column in range(column_tiles):
            number = tile * column_tiles + column
            lanes = pl.ds(column * LANES, LANES)
            slot = work.at[number % 2]
            for start in range(near):
                value = butterfly(
                    jnp.stack(
                        [
                            block[pl.ds((start + near * step) * lines + number * SUBLANES, SUBLANES), :]
                            for step in range(far)
                        ]
                    )
                )
                for step in range(far):
                    slot[start + near * step] = value[step]
            for step in range(far):
                group = pl.ds(near * step, near)
                value = butterfly(slot[group]) * chosen[tile, group]
                high, low = split2(value.reshape(near * SUBLANES, LANES))
                rows = pl.ds(tile * depth + near * SUBLANES * step, near * SUBLANES)
                parts[rows, lanes] = high
                parts[rows, pl.ds(columns + column * LANES, LANES)] = low
    half = columns // 2
    product = lambda left, right: lax.dot_general(
        left, right, (((0,), (0,)), ((), ())), preferred_element_type=jnp.float32
    )
    top = product(parts[:, :half], parts[...])
    bottom = product(parts[:, half:columns], parts[:, half:])
    high = [top[:, :half], top[:, half:columns], bottom[:, :half]]
    cross = [top[:, columns : columns + half], top[:, columns + half :], bottom[:, half:columns], bottom[:, columns:]]
    middle = high[1] + (cross[1] + cross[2].T)
    gram = scale * jnp.concatenate(
        [
            jnp.concatenate([high[0] + (cross[0] + cross[0].T), middle], axis=1),
            jnp.concatenate([middle.T, high[2] + (cross[3] + cross[3].T)], axis=1),
        ],
        axis=0,
    )
    pairs = gram.reshape(columns // 16, 2, 8, columns)
    first, second = pairs[:, 0], pairs[:, 1]
    upper = lax.broadcasted_iota(jnp.int32, first.shape, 1) < 4
    flat = lambda value: value.reshape(columns // 2, columns)
    turn = lambda value: pltpu.roll(value, 4, 1)
    zero = flat(jnp.where(upper, first, turn(second)))
    one = flat(jnp.where(upper, turn(first), second))
    here = core[0] == 0
    mine[...] = jnp.where(here, zero, one)
    other[...] = jnp.where(here, one, zero)


def local_gram(block, core, devices, columns, scale):
    lines = block.shape[0] // devices
    tiles = lines * LANES // columns // SUBLANES
    half = jax.ShapeDtypeStruct((columns // 2, columns), jnp.float32)
    vmem = pl.BlockSpec(memory_space=pltpu.VMEM)
    return pl.pallas_call(
        lambda *refs: gram_kernel(scale, devices, *refs),
        out_shape=(half, half),
        in_specs=[pl.BlockSpec(memory_space=pltpu.SMEM), vmem],
        out_specs=(vmem, vmem),
        scratch_shapes=[
            pltpu.VMEM((tiles, devices, SUBLANES, LANES), jnp.float32),
            pltpu.VMEM((2, devices, SUBLANES, LANES), jnp.float32),
            pltpu.VMEM((tiles * devices * SUBLANES, 2 * columns), jnp.bfloat16),
        ],
        compiler_params=pltpu.CompilerParams(vmem_limit_bytes=VMEM_BYTES),
        cost_estimate=pl.CostEstimate(
            flops=4 * tiles * SUBLANES * devices * columns * columns,
            bytes_accessed=4 * devices * lines * LANES,
            transcendentals=0,
        ),
        name="local_gram",
    )(core.reshape(1), block)


def local(matrix, sign_flips, sampled_rows):
    rows, columns = matrix.shape
    devices = lax.axis_size(AXES)
    chips = devices // 2
    samples = sampled_rows.shape[0] * devices
    scale = 1.0 / (rows * devices) / samples

    core = lax.axis_index("c")
    mixed = local_mix(matrix, sign_flips, sampled_rows, devices)
    mixed, core = lax.optimization_barrier((mixed, core))
    lines = mixed.shape[0] // devices
    blocks = lax.all_to_all(mixed.reshape(devices, lines * LANES), AXES, 0, 0, tiled=True)
    mine, other = local_gram(blocks.reshape(devices * lines, LANES), core, devices, columns, scale)

    summed = mine + lax.ppermute(other, "c", [(0, 1), (1, 0)])
    pieces = lax.all_to_all(summed.reshape(chips, -1, columns), CHIPS, 0, 0, tiled=True)
    return jnp.sum(pieces, axis=0)


def solution(mesh):
    fine = Mesh(mesh.devices.reshape(2, 4, 4, 2, 2), AXES)
    return jax.shard_map(
        local, mesh=fine, in_specs=(P(AXES, None), P(AXES), P(AXES)), out_specs=P(AXES, None), check_vma=False
    )
```

```python
import jax
import jax.numpy as jnp
from jax import lax
from jax.experimental import pallas as pl
from jax.experimental.pallas import tpu as pltpu
from jax.sharding import Mesh, PartitionSpec as P

AXIS = "d"
TILE = 128
LANES = 128
SUBLANES = 8
VMEM_BYTES = 32 << 20


def butterfly(value):
    count = value.shape[0]
    if count == 1:
        return value
    half = count // 2
    first, second = value[:half], value[half:]
    return jnp.concatenate([butterfly(first + second), butterfly(first - second)])


def split2(value):
    high = value.astype(jnp.bfloat16)
    low = (value - high.astype(jnp.float32)).astype(jnp.bfloat16)
    return high, low


def split3(value):
    high = value.astype(jnp.bfloat16)
    rest = value - high.astype(jnp.float32)
    middle = rest.astype(jnp.bfloat16)
    low = (rest - middle.astype(jnp.float32)).astype(jnp.bfloat16)
    return high, middle, low


def sign_table():
    row = lax.broadcasted_iota(jnp.int32, (TILE, TILE), 0)
    column = lax.broadcasted_iota(jnp.int32, (TILE, TILE), 1)
    shared = row & column
    shared = shared ^ (shared >> 4)
    shared = shared ^ (shared >> 2)
    shared = shared ^ (shared >> 1)
    return (1 - 2 * (shared & 1)).astype(jnp.float32)


def flag_lines(offsets, devices, inner):
    count = offsets.shape[1]
    place = lax.broadcasted_iota(jnp.int32, (devices, count), 0)
    left = jnp.where(place == offsets // inner, 1.0, 0.0)
    lane = lax.broadcasted_iota(jnp.int32, (LANES, count), 0)
    right = jnp.where(lane == offsets % inner, 1.0, 0.0)
    return lax.dot_general(
        left.astype(jnp.bfloat16),
        right.astype(jnp.bfloat16),
        (((1,), (1,)), ((), ())),
        preferred_element_type=jnp.float32,
    )


def mix_kernel(devices, signs_far, sampled_far, block, mixed, held, signs, sampled, arrive, small):
    groups, _, columns = block.shape
    inner = groups * TILE // devices
    lines = mixed.shape[0] // devices
    column_tiles = columns // LANES
    quarter = groups // arrive.shape[0]
    signs_copy = pltpu.make_async_copy(signs_far, signs, small.at[0])
    sampled_copy = pltpu.make_async_copy(sampled_far, sampled, small.at[1])
    incoming = [
        pltpu.make_async_copy(block.at[pl.ds(start, quarter)], held.at[pl.ds(start, quarter)], arrive.at[number])
        for number, start in enumerate(range(0, groups, quarter))
    ]
    for copy in [signs_copy, sampled_copy] + incoming:
        copy.start()
    table = sign_table()
    signs_copy.wait()
    flips = signs[...].astype(jnp.float32)
    due = {0: incoming[:1], quarter: incoming[1:-1], groups - quarter: incoming[-1:]}
    for g in range(groups):
        for copy in due.get(g, []):
            copy.wait()
        left = (table * flips[g : g + 1, :]).astype(jnp.bfloat16)
        high, middle, low = split3(held[g])
        held[g] = jnp.dot(left, low, preferred_element_type=jnp.float32) + jnp.dot(
            jnp.concatenate([left, left], axis=1),
            jnp.concatenate([middle, high], axis=0),
            preferred_element_type=jnp.float32,
        )
    sampled_copy.wait()
    offsets = jnp.concatenate([sampled[i : i + 1, :] for i in range(sampled.shape[0])], axis=1)
    flags = flag_lines(offsets, devices, inner)
    for number in range(devices):
        mixed[pl.ds(number * lines + lines - 1, 1), :] = flags[number : number + 1, :]
    for start in range(0, TILE, SUBLANES):
        for column in range(column_tiles):
            value = butterfly(held[:, pl.ds(start, SUBLANES), pl.ds(column * LANES, LANES)])
            tile = (start % inner) // SUBLANES * column_tiles + column
            for g in range(groups):
                first = (g * TILE + start) // inner * lines + tile * SUBLANES
                mixed[pl.ds(first, SUBLANES), :] = value[g]


def local_mix(matrix, signs, sampled, devices):
    rows, columns = matrix.shape
    groups = rows // TILE
    lines = rows // devices * columns // LANES + 1
    far = pl.BlockSpec(memory_space=pltpu.HBM)
    stay = lambda value: pltpu.with_memory_space_constraint(value, pltpu.HBM)
    return pl.pallas_call(
        lambda *refs: mix_kernel(devices, *refs),
        out_shape=pltpu.VMEM((devices * lines, LANES), jnp.float32),
        in_specs=[far, far, far],
        out_specs=pl.BlockSpec(memory_space=pltpu.VMEM),
        scratch_shapes=[
            pltpu.VMEM((groups, TILE, columns), jnp.float32),
            pltpu.VMEM((rows // LANES, LANES), jnp.int32),
            pltpu.VMEM((sampled.shape[0] // LANES, LANES), jnp.int32),
            pltpu.SemaphoreType.DMA((4,)),
            pltpu.SemaphoreType.DMA((2,)),
        ],
        compiler_params=pltpu.CompilerParams(vmem_limit_bytes=VMEM_BYTES),
        cost_estimate=pl.CostEstimate(
            flops=6 * rows * TILE * columns, bytes_accessed=8 * rows * columns, transcendentals=0
        ),
        name="local_mix",
    )(
        stay(signs.reshape(-1, LANES)),
        stay(sampled.reshape(-1, LANES)),
        stay(matrix.reshape(groups, TILE, columns)),
    )


def gram_kernel(scale, devices, side, block, mine, other, chosen, work, parts):
    lines = block.shape[0] // devices
    columns = mine.shape[2]
    column_tiles = columns // LANES
    tiles = lines // SUBLANES // column_tiles
    near = SUBLANES
    far = devices // near
    sublane = lax.broadcasted_iota(jnp.int32, (SUBLANES, LANES), 0)
    lane = lax.broadcasted_iota(jnp.int32, (SUBLANES, LANES), 1)
    spread = [
        jnp.broadcast_to(block[pl.ds(number * lines + lines - 1, 1), :], (SUBLANES, LANES))
        for number in range(devices)
    ]
    ones = jnp.ones((LANES, LANES), jnp.bfloat16)
    for tile in range(tiles):
        own = lane == sublane + tile * SUBLANES
        flags = jnp.concatenate([jnp.where(own, value, 0.0) for value in spread]).astype(jnp.bfloat16)
        chosen[tile] = jnp.dot(flags, ones, preferred_element_type=jnp.float32).reshape(devices, SUBLANES, LANES)
    depth = devices * SUBLANES
    for tile in range(tiles):
        for column in range(column_tiles):
            number = tile * column_tiles + column
            lanes = pl.ds(column * LANES, LANES)
            slot = work.at[number % 2]
            for start in range(near):
                value = butterfly(
                    jnp.stack(
                        [
                            block[pl.ds((start + near * step) * lines + number * SUBLANES, SUBLANES), :]
                            for step in range(far)
                        ]
                    )
                )
                for step in range(far):
                    slot[start + near * step] = value[step]
            for step in range(far):
                group = pl.ds(near * step, near)
                value = butterfly(slot[group]) * chosen[tile, group]
                high, low = split2(value.reshape(near * SUBLANES, LANES))
                rows = pl.ds(tile * depth + near * SUBLANES * step, near * SUBLANES)
                parts[rows, lanes] = high
                parts[rows, pl.ds(columns + column * LANES, LANES)] = low
    half = columns // 2
    product = lambda left, right: lax.dot_general(
        left, right, (((0,), (0,)), ((), ())), preferred_element_type=jnp.float32
    )
    top = product(parts[:, :half], parts[...])
    bottom = product(parts[:, half:columns], parts[:, half:])
    high = [top[:, :half], top[:, half:columns], bottom[:, :half]]
    cross = [top[:, columns : columns + half], top[:, columns + half :], bottom[:, half:columns], bottom[:, columns:]]
    middle = high[1] + (cross[1] + cross[2].T)
    gram = scale * jnp.concatenate(
        [
            jnp.concatenate([high[0] + (cross[0] + cross[0].T), middle], axis=1),
            jnp.concatenate([middle.T, high[2] + (cross[3] + cross[3].T)], axis=1),
        ],
        axis=0,
    )
    first_side = side[0] == 0
    out_rows = mine.shape[1]
    for place, chip in enumerate(exchange_order(mine.shape[0])):
        rows = [gram[start : start + out_rows] for start in (2 * chip * out_rows, (2 * chip + 1) * out_rows)]
        mine[place] = jnp.where(first_side, rows[0], rows[1])
        other[place] = jnp.where(first_side, rows[1], rows[0])


def local_gram(block, side, devices, columns, scale):
    lines = block.shape[0] // devices
    tiles = lines * LANES // columns // SUBLANES
    half = jax.ShapeDtypeStruct((devices // 2, columns // devices, columns), jnp.float32)
    vmem = pl.BlockSpec(memory_space=pltpu.VMEM)
    return pl.pallas_call(
        lambda *refs: gram_kernel(scale, devices, *refs),
        out_shape=(half, half),
        in_specs=[pl.BlockSpec(memory_space=pltpu.SMEM), vmem],
        out_specs=(vmem, vmem),
        scratch_shapes=[
            pltpu.VMEM((tiles, devices, SUBLANES, LANES), jnp.float32),
            pltpu.VMEM((2, devices, SUBLANES, LANES), jnp.float32),
            pltpu.VMEM((tiles * devices * SUBLANES, 2 * columns), jnp.bfloat16),
        ],
        compiler_params=pltpu.CompilerParams(vmem_limit_bytes=VMEM_BYTES),
        cost_estimate=pl.CostEstimate(
            flops=4 * tiles * SUBLANES * devices * columns * columns,
            bytes_accessed=4 * devices * lines * LANES,
            transcendentals=0,
        ),
        name="local_gram",
    )(side.reshape(1), block)


def exchange_order(chips):
    return list(reversed(range(chips)))


def local(matrix, sign_flips, sampled_rows):
    rows, columns = matrix.shape
    devices = lax.axis_size(AXIS)
    chips = devices // 2
    samples = sampled_rows.shape[0] * devices
    scale = 1.0 / (rows * devices) / samples

    side = lax.axis_index(AXIS) % 2
    mixed = local_mix(matrix, sign_flips, sampled_rows, devices)
    mixed, side = lax.optimization_barrier((mixed, side))
    lines = mixed.shape[0] // devices
    blocks = lax.all_to_all(mixed.reshape(devices, lines * LANES), AXIS, 0, 0, tiled=True)
    mine, other = local_gram(blocks.reshape(devices * lines, LANES), side, devices, columns, scale)

    summed = mine + lax.ppermute(other, AXIS, [(i, i ^ 1) for i in range(devices)])
    sides = [[2 * chip + side for chip in exchange_order(chips)] for side in range(2)]
    pieces = lax.all_to_all(summed, AXIS, 0, 0, axis_index_groups=sides, tiled=True)
    return jnp.sum(pieces, axis=0)


def solution(mesh):
    flat = Mesh(mesh.devices.reshape(-1), (AXIS,))
    return jax.shard_map(
        local, mesh=flat, in_specs=(P(AXIS, None), P(AXIS), P(AXIS)), out_specs=P(AXIS, None), check_vma=False
    )
```

```python
import math

import jax
import jax.numpy as jnp
from jax import lax
from jax.experimental import pallas as pl
from jax.experimental.pallas import tpu as pltpu
from jax.sharding import Mesh, PartitionSpec as P

AXIS = "d"
TILE = 128
LANES = 128
SUBLANES = 8
VMEM_BYTES = 32 << 20


def butterfly(value):
    count = value.shape[0]
    if count == 1:
        return value
    half = count // 2
    first, second = value[:half], value[half:]
    return jnp.concatenate([butterfly(first + second), butterfly(first - second)])


def split2(value):
    high = value.astype(jnp.bfloat16)
    low = (value - high.astype(jnp.float32)).astype(jnp.bfloat16)
    return high, low


def split3(value):
    high = value.astype(jnp.bfloat16)
    rest = value - high.astype(jnp.float32)
    middle = rest.astype(jnp.bfloat16)
    low = (rest - middle.astype(jnp.float32)).astype(jnp.bfloat16)
    return high, middle, low


def sign_table():
    row = lax.broadcasted_iota(jnp.int32, (TILE, TILE), 0)
    column = lax.broadcasted_iota(jnp.int32, (TILE, TILE), 1)
    shared = row & column
    shared = shared ^ (shared >> 4)
    shared = shared ^ (shared >> 2)
    shared = shared ^ (shared >> 1)
    return (1 - 2 * (shared & 1)).astype(jnp.float32)


def flag_lines(offsets, devices, inner):
    count = offsets.shape[1]
    place = lax.broadcasted_iota(jnp.int32, (devices, count), 0)
    left = jnp.where(place == offsets // inner, 1.0, 0.0)
    lane = lax.broadcasted_iota(jnp.int32, (LANES, count), 0)
    right = jnp.where(lane == offsets % inner, 1.0, 0.0)
    return lax.dot_general(
        left.astype(jnp.bfloat16),
        right.astype(jnp.bfloat16),
        (((1,), (1,)), ((), ())),
        preferred_element_type=jnp.float32,
    )


def mix_kernel(devices, factor, signs_far, sampled_far, block, mixed, held, signs, sampled, arrive, small):
    groups, _, columns = block.shape
    inner = groups * TILE // devices
    lines = mixed.shape[0] // devices
    column_tiles = columns // LANES
    quarter = groups // arrive.shape[0]
    signs_copy = pltpu.make_async_copy(signs_far, signs, small.at[0])
    sampled_copy = pltpu.make_async_copy(sampled_far, sampled, small.at[1])
    incoming = [
        pltpu.make_async_copy(block.at[pl.ds(start, quarter)], held.at[pl.ds(start, quarter)], arrive.at[number])
        for number, start in enumerate(range(0, groups, quarter))
    ]
    for copy in [signs_copy, sampled_copy] + incoming:
        copy.start()
    table = sign_table() * factor
    signs_copy.wait()
    flips = signs[...].astype(jnp.float32)
    due = {0: incoming[:1], quarter: incoming[1:-1], groups - quarter: incoming[-1:]}
    for g in range(groups):
        for copy in due.get(g, []):
            copy.wait()
        left = (table * flips[g : g + 1, :]).astype(jnp.bfloat16)
        high, middle, low = split3(held[g])
        held[g] = jnp.dot(left, low, preferred_element_type=jnp.float32) + jnp.dot(
            jnp.concatenate([left, left], axis=1),
            jnp.concatenate([middle, high], axis=0),
            preferred_element_type=jnp.float32,
        )
    sampled_copy.wait()
    offsets = jnp.concatenate([sampled[i : i + 1, :] for i in range(sampled.shape[0])], axis=1)
    flags = flag_lines(offsets, devices, inner)
    for number in range(devices):
        mixed[pl.ds(number * lines + lines - 1, 1), :] = flags[number : number + 1, :]
    for start in range(0, TILE, SUBLANES):
        for column in range(column_tiles):
            value = butterfly(held[:, pl.ds(start, SUBLANES), pl.ds(column * LANES, LANES)])
            tile = (start % inner) // SUBLANES * column_tiles + column
            for g in range(groups):
                first = (g * TILE + start) // inner * lines + tile * SUBLANES
                mixed[pl.ds(first, SUBLANES), :] = value[g]


def local_mix(matrix, signs, sampled, devices, factor):
    rows, columns = matrix.shape
    groups = rows // TILE
    lines = rows // devices * columns // LANES + 1
    far = pl.BlockSpec(memory_space=pltpu.HBM)
    stay = lambda value: pltpu.with_memory_space_constraint(value, pltpu.HBM)
    return pl.pallas_call(
        lambda *refs: mix_kernel(devices, factor, *refs),
        out_shape=pltpu.VMEM((devices * lines, LANES), jnp.float32),
        in_specs=[far, far, far],
        out_specs=pl.BlockSpec(memory_space=pltpu.VMEM),
        scratch_shapes=[
            pltpu.VMEM((groups, TILE, columns), jnp.float32),
            pltpu.VMEM((rows // LANES, LANES), jnp.int32),
            pltpu.VMEM((sampled.shape[0] // LANES, LANES), jnp.int32),
            pltpu.SemaphoreType.DMA((4,)),
            pltpu.SemaphoreType.DMA((2,)),
        ],
        compiler_params=pltpu.CompilerParams(vmem_limit_bytes=VMEM_BYTES),
        cost_estimate=pl.CostEstimate(
            flops=6 * rows * TILE * columns, bytes_accessed=8 * rows * columns, transcendentals=0
        ),
        name="local_mix",
    )(
        stay(signs.reshape(-1, LANES)),
        stay(sampled.reshape(-1, LANES)),
        stay(matrix.reshape(groups, TILE, columns)),
    )


def gram_kernel(scale, devices, side, block, mine, other, chosen, work, parts):
    lines = block.shape[0] // devices
    columns = mine.shape[2]
    column_tiles = columns // LANES
    tiles = lines // SUBLANES // column_tiles
    near = SUBLANES
    far = devices // near
    sublane = lax.broadcasted_iota(jnp.int32, (SUBLANES, LANES), 0)
    lane = lax.broadcasted_iota(jnp.int32, (SUBLANES, LANES), 1)
    spread = [
        jnp.broadcast_to(block[pl.ds(number * lines + lines - 1, 1), :], (SUBLANES, LANES))
        for number in range(devices)
    ]
    ones = jnp.ones((LANES, LANES), jnp.bfloat16)
    for tile in range(tiles):
        own = lane == sublane + tile * SUBLANES
        flags = jnp.concatenate([jnp.where(own, value, 0.0) for value in spread]).astype(jnp.bfloat16)
        chosen[tile] = jnp.dot(flags, ones, preferred_element_type=jnp.float32).reshape(devices, SUBLANES, LANES)
    depth = devices * SUBLANES
    for tile in range(tiles):
        for column in range(column_tiles):
            number = tile * column_tiles + column
            lanes = pl.ds(column * LANES, LANES)
            slot = work.at[number % 2]
            for start in range(near):
                value = butterfly(
                    jnp.stack(
                        [
                            block[pl.ds((start + near * step) * lines + number * SUBLANES, SUBLANES), :]
                            for step in range(far)
                        ]
                    )
                )
                for step in range(far):
                    slot[start + near * step] = value[step]
            for step in range(far):
                group = pl.ds(near * step, near)
                value = jnp.where(chosen[tile, group] != 0.0, butterfly(slot[group]), 0.0)
                high, low = split2(value.reshape(near * SUBLANES, LANES))
                rows = pl.ds(tile * depth + near * SUBLANES * step, near * SUBLANES)
                parts[rows, lanes] = high
                parts[rows, pl.ds(columns + column * LANES, LANES)] = low
    half = columns // 2
    product = lambda left, right: lax.dot_general(
        left, right, (((0,), (0,)), ((), ())), preferred_element_type=jnp.float32
    )
    top = product(parts[:, :half], parts[...])
    bottom = product(parts[:, half:columns], parts[:, half:])
    high = [top[:, :half], top[:, half:columns], bottom[:, :half]]
    cross = [top[:, columns : columns + half], top[:, columns + half :], bottom[:, half:columns], bottom[:, columns:]]
    middle = high[1] + (cross[1] + cross[2].T)
    gram = scale * jnp.concatenate(
        [
            jnp.concatenate([high[0] + (cross[0] + cross[0].T), middle], axis=1),
            jnp.concatenate([middle.T, high[2] + (cross[3] + cross[3].T)], axis=1),
        ],
        axis=0,
    )
    first_side = side[0] == 0
    out_rows = mine.shape[1]
    for place, chip in enumerate(exchange_order(mine.shape[0])):
        rows = [gram[start : start + out_rows] for start in (2 * chip * out_rows, (2 * chip + 1) * out_rows)]
        mine[place] = jnp.where(first_side, rows[0], rows[1])
        other[place] = jnp.where(first_side, rows[1], rows[0])


def local_gram(block, side, devices, columns, scale):
    lines = block.shape[0] // devices
    tiles = lines * LANES // columns // SUBLANES
    half = jax.ShapeDtypeStruct((devices // 2, columns // devices, columns), jnp.float32)
    vmem = pl.BlockSpec(memory_space=pltpu.VMEM)
    return pl.pallas_call(
        lambda *refs: gram_kernel(scale, devices, *refs),
        out_shape=(half, half),
        in_specs=[pl.BlockSpec(memory_space=pltpu.SMEM), vmem],
        out_specs=(vmem, vmem),
        scratch_shapes=[
            pltpu.VMEM((tiles, devices, SUBLANES, LANES), jnp.float32),
            pltpu.VMEM((2, devices, SUBLANES, LANES), jnp.float32),
            pltpu.VMEM((tiles * devices * SUBLANES, 2 * columns), jnp.bfloat16),
        ],
        compiler_params=pltpu.CompilerParams(vmem_limit_bytes=VMEM_BYTES),
        cost_estimate=pl.CostEstimate(
            flops=4 * tiles * SUBLANES * devices * columns * columns,
            bytes_accessed=4 * devices * lines * LANES,
            transcendentals=0,
        ),
        name="local_gram",
    )(side.reshape(1), block)


def exchange_order(chips):
    return list(reversed(range(chips)))


def local(matrix, sign_flips, sampled_rows):
    rows, columns = matrix.shape
    devices = lax.axis_size(AXIS)
    chips = devices // 2
    samples = sampled_rows.shape[0] * devices
    factor = 1.0 / math.sqrt(rows * devices)
    scale = 1.0 / samples

    side = lax.axis_index(AXIS) % 2
    mixed = local_mix(matrix, sign_flips, sampled_rows, devices, factor)
    mixed, side = lax.optimization_barrier((mixed, side))
    lines = mixed.shape[0] // devices
    blocks = lax.all_to_all(mixed.reshape(devices, lines * LANES), AXIS, 0, 0, tiled=True)
    mine, other = local_gram(blocks.reshape(devices * lines, LANES), side, devices, columns, scale)

    summed = mine + lax.ppermute(other, AXIS, [(i, i ^ 1) for i in range(devices)])
    sides = [[2 * chip + side for chip in exchange_order(chips)] for side in range(2)]
    pieces = lax.all_to_all(summed, AXIS, 0, 0, axis_index_groups=sides, tiled=True)
    return jnp.sum(pieces, axis=0)


def solution(mesh):
    flat = Mesh(mesh.devices.reshape(-1), (AXIS,))
    return jax.shard_map(
        local, mesh=flat, in_specs=(P(AXIS, None), P(AXIS), P(AXIS)), out_specs=P(AXIS, None), check_vma=False
    )
```

```python
import math

import jax
import jax.numpy as jnp
from jax import lax
from jax.experimental import pallas as pl
from jax.experimental.pallas import tpu as pltpu
from jax.sharding import Mesh, PartitionSpec as P

AXIS = "d"
TILE = 128
LANES = 128
SUBLANES = 8
VMEM_BYTES = 32 << 20


def butterfly(value):
    count = value.shape[0]
    if count == 1:
        return value
    half = count // 2
    first, second = value[:half], value[half:]
    return jnp.concatenate([butterfly(first + second), butterfly(first - second)])


def split2(value):
    high = value.astype(jnp.bfloat16)
    low = (value - high.astype(jnp.float32)).astype(jnp.bfloat16)
    return high, low


def split3(value):
    high = value.astype(jnp.bfloat16)
    rest = value - high.astype(jnp.float32)
    middle = rest.astype(jnp.bfloat16)
    low = (rest - middle.astype(jnp.float32)).astype(jnp.bfloat16)
    return high, middle, low


def sign_table():
    row = lax.broadcasted_iota(jnp.int32, (TILE, TILE), 0)
    column = lax.broadcasted_iota(jnp.int32, (TILE, TILE), 1)
    shared = row & column
    shared = shared ^ (shared >> 4)
    shared = shared ^ (shared >> 2)
    shared = shared ^ (shared >> 1)
    return (1 - 2 * (shared & 1)).astype(jnp.float32)


def flag_lines(offsets, devices, inner):
    count = offsets.shape[1]
    place = lax.broadcasted_iota(jnp.int32, (devices, count), 0)
    left = jnp.where(place == offsets // inner, 1.0, 0.0)
    lane = lax.broadcasted_iota(jnp.int32, (LANES, count), 0)
    right = jnp.where(lane == offsets % inner, 1.0, 0.0)
    return lax.dot_general(
        left.astype(jnp.bfloat16),
        right.astype(jnp.bfloat16),
        (((1,), (1,)), ((), ())),
        preferred_element_type=jnp.float32,
    )


def mix_kernel(devices, factor, signs_far, sampled_far, block, mixed, held, signs, sampled, arrive, small):
    groups, _, columns = block.shape
    inner = groups * TILE // devices
    lines = mixed.shape[0] // devices
    column_tiles = columns // LANES
    quarter = groups // arrive.shape[0]
    signs_copy = pltpu.make_async_copy(signs_far, signs, small.at[0])
    sampled_copy = pltpu.make_async_copy(sampled_far, sampled, small.at[1])
    incoming = [
        pltpu.make_async_copy(block.at[pl.ds(start, quarter)], held.at[pl.ds(start, quarter)], arrive.at[number])
        for number, start in enumerate(range(0, groups, quarter))
    ]
    for copy in [signs_copy, sampled_copy] + incoming:
        copy.start()
    table = sign_table() * factor
    signs_copy.wait()
    flips = signs[...].astype(jnp.float32)
    due = {0: incoming[:1], quarter: incoming[1:-1], groups - quarter: incoming[-1:]}
    for g in range(groups):
        for copy in due.get(g, []):
            copy.wait()
        left = (table * flips[g : g + 1, :]).astype(jnp.bfloat16)
        high, middle, low = split3(held[g])
        held[g] = jnp.dot(left, low, preferred_element_type=jnp.float32) + jnp.dot(
            jnp.concatenate([left, left], axis=1),
            jnp.concatenate([middle, high], axis=0),
            preferred_element_type=jnp.float32,
        )
    sampled_copy.wait()
    offsets = jnp.concatenate([sampled[i : i + 1, :] for i in range(sampled.shape[0])], axis=1)
    flags = flag_lines(offsets, devices, inner)
    for number in range(devices):
        mixed[pl.ds(number * lines + lines - 1, 1), :] = flags[number : number + 1, :]
    for start in range(0, TILE, SUBLANES):
        for column in range(column_tiles):
            value = butterfly(held[:, pl.ds(start, SUBLANES), pl.ds(column * LANES, LANES)])
            tile = (start % inner) // SUBLANES * column_tiles + column
            for g in range(groups):
                first = (g * TILE + start) // inner * lines + tile * SUBLANES
                mixed[pl.ds(first, SUBLANES), :] = value[g]


def local_mix(matrix, signs, sampled, devices, factor):
    rows, columns = matrix.shape
    groups = rows // TILE
    lines = rows // devices * columns // LANES + 1
    far = pl.BlockSpec(memory_space=pltpu.HBM)
    stay = lambda value: pltpu.with_memory_space_constraint(value, pltpu.HBM)
    return pl.pallas_call(
        lambda *refs: mix_kernel(devices, factor, *refs),
        out_shape=pltpu.VMEM((devices * lines, LANES), jnp.float32),
        in_specs=[far, far, far],
        out_specs=pl.BlockSpec(memory_space=pltpu.VMEM),
        scratch_shapes=[
            pltpu.VMEM((groups, TILE, columns), jnp.float32),
            pltpu.VMEM((rows // LANES, LANES), jnp.int32),
            pltpu.VMEM((sampled.shape[0] // LANES, LANES), jnp.int32),
            pltpu.SemaphoreType.DMA((4,)),
            pltpu.SemaphoreType.DMA((2,)),
        ],
        compiler_params=pltpu.CompilerParams(vmem_limit_bytes=VMEM_BYTES),
        cost_estimate=pl.CostEstimate(
            flops=6 * rows * TILE * columns, bytes_accessed=8 * rows * columns, transcendentals=0
        ),
        name="local_mix",
    )(
        stay(signs.reshape(-1, LANES)),
        stay(sampled.reshape(-1, LANES)),
        stay(matrix.reshape(groups, TILE, columns)),
    )


def gram_kernel(scale, devices, side, block, mine, other, chosen, work, parts):
    lines = block.shape[0] // devices
    columns = mine.shape[2]
    column_tiles = columns // LANES
    tiles = lines // SUBLANES // column_tiles
    near = SUBLANES
    far = devices // near
    sublane = lax.broadcasted_iota(jnp.int32, (SUBLANES, LANES), 0)
    lane = lax.broadcasted_iota(jnp.int32, (SUBLANES, LANES), 1)
    spread = [
        jnp.broadcast_to(block[pl.ds(number * lines + lines - 1, 1), :], (SUBLANES, LANES))
        for number in range(devices)
    ]
    ones = jnp.ones((LANES, LANES), jnp.bfloat16)
    for tile in range(tiles):
        own = lane == sublane + tile * SUBLANES
        flags = jnp.concatenate([jnp.where(own, value, 0.0) for value in spread]).astype(jnp.bfloat16)
        chosen[tile] = jnp.dot(flags, ones, preferred_element_type=jnp.float32).reshape(devices, SUBLANES, LANES)
    depth = devices * SUBLANES
    for tile in range(tiles):
        for column in range(column_tiles):
            number = tile * column_tiles + column
            lanes = pl.ds(column * LANES, LANES)
            slot = work.at[number % 2]
            for start in range(near):
                value = butterfly(
                    jnp.stack(
                        [
                            block[pl.ds((start + near * step) * lines + number * SUBLANES, SUBLANES), :]
                            for step in range(far)
                        ]
                    )
                )
                for step in range(far):
                    slot[start + near * step] = value[step]
            for step in range(far):
                group = pl.ds(near * step, near)
                value = jnp.where(chosen[tile, group] != 0.0, butterfly(slot[group]), 0.0)
                high, low = split2(value.reshape(near * SUBLANES, LANES))
                rows = pl.ds(tile * depth + near * SUBLANES * step, near * SUBLANES)
                parts[rows, lanes] = high
                parts[rows, pl.ds(columns + column * LANES, LANES)] = low
    half = columns // 2
    product = lambda left, right: lax.dot_general(
        left, right, (((0,), (0,)), ((), ())), preferred_element_type=jnp.float32
    )
    top = product(parts[:, :half], parts[...])
    bottom = product(parts[:, half:columns], parts[:, half:])
    high = [top[:, :half], top[:, half:columns], bottom[:, :half]]
    cross = [top[:, columns : columns + half], top[:, columns + half :], bottom[:, half:columns], bottom[:, columns:]]
    middle = high[1] + (cross[1] + cross[2].T)
    gram = scale * jnp.concatenate(
        [
            jnp.concatenate([high[0] + (cross[0] + cross[0].T), middle], axis=1),
            jnp.concatenate([middle.T, high[2] + (cross[3] + cross[3].T)], axis=1),
        ],
        axis=0,
    )
    first_side = side[0] == 0
    out_rows = mine.shape[1]
    for place, chip in enumerate(exchange_order(mine.shape[0])):
        rows = [gram[start : start + out_rows] for start in (2 * chip * out_rows, (2 * chip + 1) * out_rows)]
        mine[place] = jnp.where(first_side, rows[0], rows[1])
        other[place] = jnp.where(first_side, rows[1], rows[0])


def local_gram(block, side, devices, columns, scale):
    lines = block.shape[0] // devices
    tiles = lines * LANES // columns // SUBLANES
    half = jax.ShapeDtypeStruct((devices // 2, columns // devices, columns), jnp.float32)
    vmem = pl.BlockSpec(memory_space=pltpu.VMEM)
    return pl.pallas_call(
        lambda *refs: gram_kernel(scale, devices, *refs),
        out_shape=(half, half),
        in_specs=[pl.BlockSpec(memory_space=pltpu.SMEM), vmem],
        out_specs=(vmem, vmem),
        scratch_shapes=[
            pltpu.VMEM((tiles, devices, SUBLANES, LANES), jnp.float32),
            pltpu.VMEM((2, devices, SUBLANES, LANES), jnp.float32),
            pltpu.VMEM((tiles * devices * SUBLANES, 2 * columns), jnp.bfloat16),
        ],
        compiler_params=pltpu.CompilerParams(vmem_limit_bytes=VMEM_BYTES),
        cost_estimate=pl.CostEstimate(
            flops=4 * tiles * SUBLANES * devices * columns * columns,
            bytes_accessed=4 * devices * lines * LANES,
            transcendentals=0,
        ),
        name="local_gram",
    )(side.reshape(1), block)


def exchange_order(chips):
    return [place ^ 0b010101 for place in range(chips)]


def local(matrix, sign_flips, sampled_rows):
    rows, columns = matrix.shape
    devices = lax.axis_size(AXIS)
    chips = devices // 2
    samples = sampled_rows.shape[0] * devices
    factor = 1.0 / math.sqrt(rows * devices)
    scale = 1.0 / samples

    side = lax.axis_index(AXIS) % 2
    mixed = local_mix(matrix, sign_flips, sampled_rows, devices, factor)
    mixed, side = lax.optimization_barrier((mixed, side))
    lines = mixed.shape[0] // devices
    blocks = lax.all_to_all(mixed.reshape(devices, lines * LANES), AXIS, 0, 0, tiled=True)
    mine, other = local_gram(blocks.reshape(devices * lines, LANES), side, devices, columns, scale)

    summed = mine + lax.ppermute(other, AXIS, [(i, i ^ 1) for i in range(devices)])
    sides = [[2 * chip + side for chip in exchange_order(chips)] for side in range(2)]
    pieces = lax.all_to_all(summed, AXIS, 0, 0, axis_index_groups=sides, tiled=True)
    return jnp.sum(pieces, axis=0)


def solution(mesh):
    flat = Mesh(mesh.devices.reshape(-1), (AXIS,))
    return jax.shard_map(
        local, mesh=flat, in_specs=(P(AXIS, None), P(AXIS), P(AXIS)), out_specs=P(AXIS, None), check_vma=False
    )
```

```python
import math

import jax
import jax.numpy as jnp
from jax import lax
from jax.experimental import pallas as pl
from jax.experimental.pallas import tpu as pltpu
from jax.sharding import Mesh, PartitionSpec as P

AXIS = "d"
TILE = 128
LANES = 128
SUBLANES = 8
VMEM_BYTES = 32 << 20


def butterfly(value):
    count = value.shape[0]
    if count == 1:
        return value
    half = count // 2
    first, second = value[:half], value[half:]
    return jnp.concatenate([butterfly(first + second), butterfly(first - second)])


def split2(value):
    high = value.astype(jnp.bfloat16)
    low = (value - high.astype(jnp.float32)).astype(jnp.bfloat16)
    return high, low


def split3(value):
    high = value.astype(jnp.bfloat16)
    rest = value - high.astype(jnp.float32)
    middle = rest.astype(jnp.bfloat16)
    low = (rest - middle.astype(jnp.float32)).astype(jnp.bfloat16)
    return high, middle, low


def sign_table():
    row = lax.broadcasted_iota(jnp.int32, (TILE, TILE), 0)
    column = lax.broadcasted_iota(jnp.int32, (TILE, TILE), 1)
    shared = row & column
    shared = shared ^ (shared >> 4)
    shared = shared ^ (shared >> 2)
    shared = shared ^ (shared >> 1)
    return (1 - 2 * (shared & 1)).astype(jnp.float32)


def flag_lines(offsets, devices, inner):
    count = offsets.shape[1]
    place = lax.broadcasted_iota(jnp.int32, (devices, count), 0)
    left = jnp.where(place == offsets // inner, 1.0, 0.0)
    lane = lax.broadcasted_iota(jnp.int32, (LANES, count), 0)
    right = jnp.where(lane == offsets % inner, 1.0, 0.0)
    return lax.dot_general(
        left.astype(jnp.bfloat16),
        right.astype(jnp.bfloat16),
        (((1,), (1,)), ((), ())),
        preferred_element_type=jnp.float32,
    )


def mix_kernel(devices, factor, signs_far, sampled_far, block, mixed, held, signs, sampled, arrive, small):
    groups, _, columns = block.shape
    inner = groups * TILE // devices
    lines = mixed.shape[0] // devices
    column_tiles = columns // LANES
    place = places(main_order(devices))
    quarter = groups // arrive.shape[0]
    signs_copy = pltpu.make_async_copy(signs_far, signs, small.at[0])
    sampled_copy = pltpu.make_async_copy(sampled_far, sampled, small.at[1])
    incoming = [
        pltpu.make_async_copy(block.at[pl.ds(start, quarter)], held.at[pl.ds(start, quarter)], arrive.at[number])
        for number, start in enumerate(range(0, groups, quarter))
    ]
    for copy in [signs_copy, sampled_copy] + incoming:
        copy.start()
    table = sign_table() * factor
    signs_copy.wait()
    flips = signs[...].astype(jnp.float32)
    due = {0: incoming[:1], quarter: incoming[1:-1], groups - quarter: incoming[-1:]}
    for g in range(groups):
        for copy in due.get(g, []):
            copy.wait()
        left = (table * flips[g : g + 1, :]).astype(jnp.bfloat16)
        high, middle, low = split3(held[g])
        held[g] = jnp.dot(left, low, preferred_element_type=jnp.float32) + jnp.dot(
            jnp.concatenate([left, left], axis=1),
            jnp.concatenate([middle, high], axis=0),
            preferred_element_type=jnp.float32,
        )
    sampled_copy.wait()
    offsets = jnp.concatenate([sampled[i : i + 1, :] for i in range(sampled.shape[0])], axis=1)
    flags = flag_lines(offsets, devices, inner)
    for number in range(devices):
        mixed[pl.ds(place[number] * lines + lines - 1, 1), :] = flags[number : number + 1, :]
    for start in range(0, TILE, SUBLANES):
        for column in range(column_tiles):
            value = butterfly(held[:, pl.ds(start, SUBLANES), pl.ds(column * LANES, LANES)])
            tile = (start % inner) // SUBLANES * column_tiles + column
            for g in range(groups):
                first = place[(g * TILE + start) // inner] * lines + tile * SUBLANES
                mixed[pl.ds(first, SUBLANES), :] = value[g]


def local_mix(matrix, signs, sampled, devices, factor):
    rows, columns = matrix.shape
    groups = rows // TILE
    lines = rows // devices * columns // LANES + 1
    far = pl.BlockSpec(memory_space=pltpu.HBM)
    stay = lambda value: pltpu.with_memory_space_constraint(value, pltpu.HBM)
    return pl.pallas_call(
        lambda *refs: mix_kernel(devices, factor, *refs),
        out_shape=pltpu.VMEM((devices * lines, LANES), jnp.float32),
        in_specs=[far, far, far],
        out_specs=pl.BlockSpec(memory_space=pltpu.VMEM),
        scratch_shapes=[
            pltpu.VMEM((groups, TILE, columns), jnp.float32),
            pltpu.VMEM((rows // LANES, LANES), jnp.int32),
            pltpu.VMEM((sampled.shape[0] // LANES, LANES), jnp.int32),
            pltpu.SemaphoreType.DMA((4,)),
            pltpu.SemaphoreType.DMA((2,)),
        ],
        compiler_params=pltpu.CompilerParams(vmem_limit_bytes=VMEM_BYTES),
        cost_estimate=pl.CostEstimate(
            flops=6 * rows * TILE * columns, bytes_accessed=8 * rows * columns, transcendentals=0
        ),
        name="local_mix",
    )(
        stay(signs.reshape(-1, LANES)),
        stay(sampled.reshape(-1, LANES)),
        stay(matrix.reshape(groups, TILE, columns)),
    )


def gram_kernel(scale, devices, side, block, mine, other, chosen, work, parts):
    lines = block.shape[0] // devices
    columns = mine.shape[2]
    column_tiles = columns // LANES
    tiles = lines // SUBLANES // column_tiles
    near = SUBLANES
    far = devices // near
    place = places(main_order(devices))
    sublane = lax.broadcasted_iota(jnp.int32, (SUBLANES, LANES), 0)
    lane = lax.broadcasted_iota(jnp.int32, (SUBLANES, LANES), 1)
    spread = [
        jnp.broadcast_to(block[pl.ds(place[number] * lines + lines - 1, 1), :], (SUBLANES, LANES))
        for number in range(devices)
    ]
    ones = jnp.ones((LANES, LANES), jnp.bfloat16)
    for tile in range(tiles):
        own = lane == sublane + tile * SUBLANES
        flags = jnp.concatenate([jnp.where(own, value, 0.0) for value in spread]).astype(jnp.bfloat16)
        chosen[tile] = jnp.dot(flags, ones, preferred_element_type=jnp.float32).reshape(devices, SUBLANES, LANES)
    depth = devices * SUBLANES
    for tile in range(tiles):
        for column in range(column_tiles):
            number = tile * column_tiles + column
            lanes = pl.ds(column * LANES, LANES)
            slot = work.at[number % 2]
            for start in range(near):
                value = butterfly(
                    jnp.stack(
                        [
                            block[pl.ds(place[start + near * step] * lines + number * SUBLANES, SUBLANES), :]
                            for step in range(far)
                        ]
                    )
                )
                for step in range(far):
                    slot[start + near * step] = value[step]
            for step in range(far):
                group = pl.ds(near * step, near)
                value = jnp.where(chosen[tile, group] != 0.0, butterfly(slot[group]), 0.0)
                high, low = split2(value.reshape(near * SUBLANES, LANES))
                rows = pl.ds(tile * depth + near * SUBLANES * step, near * SUBLANES)
                parts[rows, lanes] = high
                parts[rows, pl.ds(columns + column * LANES, LANES)] = low
    half = columns // 2
    product = lambda left, right: lax.dot_general(
        left, right, (((0,), (0,)), ((), ())), preferred_element_type=jnp.float32
    )
    top = product(parts[:, :half], parts[...])
    bottom = product(parts[:, half:columns], parts[:, half:])
    high = [top[:, :half], top[:, half:columns], bottom[:, :half]]
    cross = [top[:, columns : columns + half], top[:, columns + half :], bottom[:, half:columns], bottom[:, columns:]]
    middle = high[1] + (cross[1] + cross[2].T)
    gram = scale * jnp.concatenate(
        [
            jnp.concatenate([high[0] + (cross[0] + cross[0].T), middle], axis=1),
            jnp.concatenate([middle.T, high[2] + (cross[3] + cross[3].T)], axis=1),
        ],
        axis=0,
    )
    first_side = side[0] == 0
    out_rows = mine.shape[1]
    for number, chip in enumerate(last_order(mine.shape[0])):
        starts = [(2 * chip + half) * out_rows for half in range(2)]
        zero, one = [gram[start : start + out_rows] for start in starts]
        mine[number] = jnp.where(first_side, zero, one)
        other[number] = jnp.where(first_side, one, zero)


def local_gram(block, side, devices, columns, scale):
    lines = block.shape[0] // devices
    tiles = lines * LANES // columns // SUBLANES
    half = jax.ShapeDtypeStruct((devices // 2, columns // devices, columns), jnp.float32)
    vmem = pl.BlockSpec(memory_space=pltpu.VMEM)
    return pl.pallas_call(
        lambda *refs: gram_kernel(scale, devices, *refs),
        out_shape=(half, half),
        in_specs=[pl.BlockSpec(memory_space=pltpu.SMEM), vmem],
        out_specs=(vmem, vmem),
        scratch_shapes=[
            pltpu.VMEM((tiles, devices, SUBLANES, LANES), jnp.float32),
            pltpu.VMEM((2, devices, SUBLANES, LANES), jnp.float32),
            pltpu.VMEM((tiles * devices * SUBLANES, 2 * columns), jnp.bfloat16),
        ],
        compiler_params=pltpu.CompilerParams(vmem_limit_bytes=VMEM_BYTES),
        cost_estimate=pl.CostEstimate(
            flops=4 * tiles * SUBLANES * devices * columns * columns,
            bytes_accessed=4 * devices * lines * LANES,
            transcendentals=0,
        ),
        name="local_gram",
    )(side.reshape(1), block)


def chip_at(x, y, z):
    return ((y % 2 * 4 + z) * 4 + x) * 2 + y // 2


def coordinates(chip):
    return chip // 2 % 4, chip % 2 * 2 + chip // 32, chip // 8 % 4


def turned(chip):
    return chip_at(*[(c + 2) % 4 for c in coordinates(chip)])


def main_order(devices):
    return [device for chip in range(devices // 2) for device in (2 * chip, 2 * turned(chip) + 1)]


def last_order(chips):
    return [turned(chip) for chip in range(chips)]


def places(order):
    return {device: place for place, device in enumerate(order)}


def local(matrix, sign_flips, sampled_rows):
    rows, columns = matrix.shape
    devices = lax.axis_size(AXIS)
    chips = devices // 2
    samples = sampled_rows.shape[0] * devices
    factor = 1.0 / math.sqrt(rows * devices)
    scale = 1.0 / samples

    side = lax.axis_index(AXIS) % 2
    mixed = local_mix(matrix, sign_flips, sampled_rows, devices, factor)
    mixed, side = lax.optimization_barrier((mixed, side))
    lines = mixed.shape[0] // devices
    blocks = lax.all_to_all(
        mixed.reshape(devices, lines * LANES), AXIS, 0, 0, axis_index_groups=[main_order(devices)], tiled=True
    )
    mine, other = local_gram(blocks.reshape(devices * lines, LANES), side, devices, columns, scale)

    summed = mine + lax.ppermute(other, AXIS, [(i, i ^ 1) for i in range(devices)])
    sides = [[2 * chip + side for chip in last_order(chips)] for side in range(2)]
    pieces = lax.all_to_all(summed, AXIS, 0, 0, axis_index_groups=sides, tiled=True)
    return jnp.sum(pieces, axis=0)


def solution(mesh):
    flat = Mesh(mesh.devices.reshape(-1), (AXIS,))
    return jax.shard_map(
        local, mesh=flat, in_specs=(P(AXIS, None), P(AXIS), P(AXIS)), out_specs=P(AXIS, None), check_vma=False
    )
```

```python
import math

import jax
import jax.numpy as jnp
from jax import lax
from jax.experimental import pallas as pl
from jax.experimental.pallas import tpu as pltpu
from jax.sharding import Mesh, PartitionSpec as P

AXIS = "d"
TILE = 128
LANES = 128
SUBLANES = 8
VMEM_BYTES = 32 << 20


def butterfly(value):
    count = value.shape[0]
    if count == 1:
        return value
    half = count // 2
    first, second = value[:half], value[half:]
    return jnp.concatenate([butterfly(first + second), butterfly(first - second)])


def split2(value):
    high = value.astype(jnp.bfloat16)
    low = (value - high.astype(jnp.float32)).astype(jnp.bfloat16)
    return high, low


def split3(value):
    high = value.astype(jnp.bfloat16)
    rest = value - high.astype(jnp.float32)
    middle = rest.astype(jnp.bfloat16)
    low = (rest - middle.astype(jnp.float32)).astype(jnp.bfloat16)
    return high, middle, low


def sign_table():
    row = lax.broadcasted_iota(jnp.int32, (TILE, TILE), 0)
    column = lax.broadcasted_iota(jnp.int32, (TILE, TILE), 1)
    shared = row & column
    shared = shared ^ (shared >> 4)
    shared = shared ^ (shared >> 2)
    shared = shared ^ (shared >> 1)
    return (1 - 2 * (shared & 1)).astype(jnp.float32)


def flag_lines(offsets, devices, inner):
    count = offsets.shape[1]
    place = lax.broadcasted_iota(jnp.int32, (devices, count), 0)
    left = jnp.where(place == offsets // inner, 1.0, 0.0)
    lane = lax.broadcasted_iota(jnp.int32, (LANES, count), 0)
    right = jnp.where(lane == offsets % inner, 1.0, 0.0)
    return lax.dot_general(
        left.astype(jnp.bfloat16),
        right.astype(jnp.bfloat16),
        (((1,), (1,)), ((), ())),
        preferred_element_type=jnp.float32,
    )


def mix_kernel(devices, factor, signs_far, sampled_far, block, mixed, held, signs, sampled, arrive, small):
    groups, _, columns = block.shape
    inner = groups * TILE // devices
    lines = mixed.shape[0] // devices
    column_tiles = columns // LANES
    place = places(main_order(devices))
    quarter = groups // arrive.shape[0]
    signs_copy = pltpu.make_async_copy(signs_far, signs, small.at[0])
    sampled_copy = pltpu.make_async_copy(sampled_far, sampled, small.at[1])
    incoming = [
        pltpu.make_async_copy(block.at[pl.ds(start, quarter)], held.at[pl.ds(start, quarter)], arrive.at[number])
        for number, start in enumerate(range(0, groups, quarter))
    ]
    for copy in [signs_copy, sampled_copy] + incoming:
        copy.start()
    table = sign_table() * factor
    signs_copy.wait()
    flips = signs[...].astype(jnp.float32)
    due = {0: incoming[:1], quarter: incoming[1:-1], groups - quarter: incoming[-1:]}
    for g in range(groups):
        for copy in due.get(g, []):
            copy.wait()
        left = (table * flips[g : g + 1, :]).astype(jnp.bfloat16)
        high, middle, low = split3(held[g])
        held[g] = jnp.dot(left, low, preferred_element_type=jnp.float32) + jnp.dot(
            jnp.concatenate([left, left], axis=1),
            jnp.concatenate([middle, high], axis=0),
            preferred_element_type=jnp.float32,
        )
    sampled_copy.wait()
    offsets = jnp.concatenate([sampled[i : i + 1, :] for i in range(sampled.shape[0])], axis=1)
    flags = flag_lines(offsets, devices, inner)
    for number in range(devices):
        mixed[pl.ds(place[number] * lines + lines - 1, 1), :] = flags[number : number + 1, :]
    for start in range(0, TILE, SUBLANES):
        for column in range(column_tiles):
            value = butterfly(held[:, pl.ds(start, SUBLANES), pl.ds(column * LANES, LANES)])
            tile = (start % inner) // SUBLANES * column_tiles + column
            for g in range(groups):
                first = place[(g * TILE + start) // inner] * lines + tile * SUBLANES
                mixed[pl.ds(first, SUBLANES), :] = value[g]


def local_mix(matrix, signs, sampled, devices, factor):
    rows, columns = matrix.shape
    groups = rows // TILE
    lines = rows // devices * columns // LANES + 1
    far = pl.BlockSpec(memory_space=pltpu.HBM)
    stay = lambda value: pltpu.with_memory_space_constraint(value, pltpu.HBM)
    return pl.pallas_call(
        lambda *refs: mix_kernel(devices, factor, *refs),
        out_shape=pltpu.VMEM((devices * lines, LANES), jnp.float32),
        in_specs=[far, far, far],
        out_specs=pl.BlockSpec(memory_space=pltpu.VMEM),
        scratch_shapes=[
            pltpu.VMEM((groups, TILE, columns), jnp.float32),
            pltpu.VMEM((rows // LANES, LANES), jnp.int32),
            pltpu.VMEM((sampled.shape[0] // LANES, LANES), jnp.int32),
            pltpu.SemaphoreType.DMA((4,)),
            pltpu.SemaphoreType.DMA((2,)),
        ],
        compiler_params=pltpu.CompilerParams(vmem_limit_bytes=VMEM_BYTES),
        cost_estimate=pl.CostEstimate(
            flops=6 * rows * TILE * columns, bytes_accessed=8 * rows * columns, transcendentals=0
        ),
        name="local_mix",
    )(
        stay(signs.reshape(-1, LANES)),
        stay(sampled.reshape(-1, LANES)),
        stay(matrix.reshape(groups, TILE, columns)),
    )


def gram_kernel(scale, devices, side, block, mine, other, chosen, work, parts):
    lines = block.shape[0] // devices
    columns = mine.shape[2]
    column_tiles = columns // LANES
    tiles = lines // SUBLANES // column_tiles
    near = SUBLANES
    far = devices // near
    place = places(main_order(devices))
    sublane = lax.broadcasted_iota(jnp.int32, (SUBLANES, LANES), 0)
    lane = lax.broadcasted_iota(jnp.int32, (SUBLANES, LANES), 1)
    spread = [
        jnp.broadcast_to(block[pl.ds(place[number] * lines + lines - 1, 1), :], (SUBLANES, LANES))
        for number in range(devices)
    ]
    ones = jnp.ones((LANES, LANES), jnp.bfloat16)
    for tile in range(tiles):
        own = lane == sublane + tile * SUBLANES
        flags = jnp.concatenate([jnp.where(own, value, 0.0) for value in spread]).astype(jnp.bfloat16)
        chosen[tile] = jnp.dot(flags, ones, preferred_element_type=jnp.float32).reshape(devices, SUBLANES, LANES)
    depth = devices * SUBLANES
    for tile in range(tiles):
        for column in range(column_tiles):
            number = tile * column_tiles + column
            lanes = pl.ds(column * LANES, LANES)
            slot = work.at[number % 2]
            for start in range(near):
                value = butterfly(
                    jnp.stack(
                        [
                            block[pl.ds(place[start + near * step] * lines + number * SUBLANES, SUBLANES), :]
                            for step in range(far)
                        ]
                    )
                )
                for step in range(far):
                    slot[start + near * step] = value[step]
            for step in range(far):
                group = pl.ds(near * step, near)
                value = jnp.where(chosen[tile, group] != 0.0, butterfly(slot[group]), 0.0)
                high, low = split2(value.reshape(near * SUBLANES, LANES))
                rows = pl.ds(tile * depth + near * SUBLANES * step, near * SUBLANES)
                parts[rows, lanes] = high
                parts[rows, pl.ds(columns + column * LANES, LANES)] = low
    half = columns // 2
    product = lambda left, right: lax.dot_general(
        left, right, (((0,), (0,)), ((), ())), preferred_element_type=jnp.float32
    )
    top = product(parts[:, :half], parts[...])
    bottom = product(parts[:, half:columns], parts[:, half:])
    high = [top[:, :half], top[:, half:columns], bottom[:, :half]]
    cross = [top[:, columns : columns + half], top[:, columns + half :], bottom[:, half:columns], bottom[:, columns:]]
    middle = high[1] + (cross[1] + cross[2].T)
    gram = scale * jnp.concatenate(
        [
            jnp.concatenate([high[0] + (cross[0] + cross[0].T), middle], axis=1),
            jnp.concatenate([middle.T, high[2] + (cross[3] + cross[3].T)], axis=1),
        ],
        axis=0,
    )
    first_side = side[0] == 0
    out_rows = mine.shape[1]
    for number, chip in enumerate(last_order(mine.shape[0])):
        starts = [(2 * chip + half) * out_rows for half in range(2)]
        zero, one = [gram[start : start + out_rows] for start in starts]
        mine[number] = jnp.where(first_side, zero, one)
        other[number] = jnp.where(first_side, one, zero)


def local_gram(block, side, devices, columns, scale):
    lines = block.shape[0] // devices
    tiles = lines * LANES // columns // SUBLANES
    half = jax.ShapeDtypeStruct((devices // 2, columns // devices, columns), jnp.float32)
    vmem = pl.BlockSpec(memory_space=pltpu.VMEM)
    return pl.pallas_call(
        lambda *refs: gram_kernel(scale, devices, *refs),
        out_shape=(half, half),
        in_specs=[pl.BlockSpec(memory_space=pltpu.SMEM), vmem],
        out_specs=(vmem, vmem),
        scratch_shapes=[
            pltpu.VMEM((tiles, devices, SUBLANES, LANES), jnp.float32),
            pltpu.VMEM((2, devices, SUBLANES, LANES), jnp.float32),
            pltpu.VMEM((tiles * devices * SUBLANES, 2 * columns), jnp.bfloat16),
        ],
        compiler_params=pltpu.CompilerParams(vmem_limit_bytes=VMEM_BYTES),
        cost_estimate=pl.CostEstimate(
            flops=4 * tiles * SUBLANES * devices * columns * columns,
            bytes_accessed=4 * devices * lines * LANES,
            transcendentals=0,
        ),
        name="local_gram",
    )(side.reshape(1), block)


def chip_at(x, y, z):
    return ((y % 2 * 4 + z) * 4 + x) * 2 + y // 2


def coordinates(chip):
    return chip // 2 % 4, chip % 2 * 2 + chip // 32, chip // 8 % 4


def turned(chip):
    return chip_at(*[(c + 2) % 4 for c in coordinates(chip)])


def main_order(devices):
    return [device for chip in range(devices // 2) for device in (2 * chip, 2 * turned(chip) + 1)]


def last_order(chips):
    order = []
    for place in range(chips):
        x, y, z = place % 4, place // 4 % 4, place // 16
        order.append(chip_at(x, (y + x) % 4, (z + y + x) % 4))
    order[0], order[53] = order[53], order[0]
    return order


def places(order):
    return {device: place for place, device in enumerate(order)}


def local(matrix, sign_flips, sampled_rows):
    rows, columns = matrix.shape
    devices = lax.axis_size(AXIS)
    chips = devices // 2
    samples = sampled_rows.shape[0] * devices
    factor = 1.0 / math.sqrt(rows * devices)
    scale = 1.0 / samples

    side = lax.axis_index(AXIS) % 2
    mixed = local_mix(matrix, sign_flips, sampled_rows, devices, factor)
    mixed, side = lax.optimization_barrier((mixed, side))
    lines = mixed.shape[0] // devices
    blocks = lax.all_to_all(
        mixed.reshape(devices, lines * LANES), AXIS, 0, 0, axis_index_groups=[main_order(devices)], tiled=True
    )
    mine, other = local_gram(blocks.reshape(devices * lines, LANES), side, devices, columns, scale)

    summed = mine + lax.ppermute(other, AXIS, [(i, i ^ 1) for i in range(devices)])
    sides = [[2 * chip + side for chip in last_order(chips)] for side in range(2)]
    pieces = lax.all_to_all(summed, AXIS, 0, 0, axis_index_groups=sides, tiled=True)
    return jnp.sum(pieces, axis=0)


def solution(mesh):
    flat = Mesh(mesh.devices.reshape(-1), (AXIS,))
    return jax.shard_map(
        local, mesh=flat, in_specs=(P(AXIS, None), P(AXIS), P(AXIS)), out_specs=P(AXIS, None), check_vma=False
    )
```

```python
import math

import jax
import jax.numpy as jnp
from jax import lax
from jax.experimental import pallas as pl
from jax.experimental.pallas import tpu as pltpu
from jax.sharding import Mesh, PartitionSpec as P

AXIS = "d"
TILE = 128
LANES = 128
SUBLANES = 8
VMEM_BYTES = 32 << 20


def butterfly(value):
    count = value.shape[0]
    if count == 1:
        return value
    half = count // 2
    first, second = value[:half], value[half:]
    return jnp.concatenate([butterfly(first + second), butterfly(first - second)])


def split2(value):
    high = value.astype(jnp.bfloat16)
    low = (value - high.astype(jnp.float32)).astype(jnp.bfloat16)
    return high, low


def split3(value):
    high = value.astype(jnp.bfloat16)
    rest = value - high.astype(jnp.float32)
    middle = rest.astype(jnp.bfloat16)
    low = (rest - middle.astype(jnp.float32)).astype(jnp.bfloat16)
    return high, middle, low


def sign_table():
    row = lax.broadcasted_iota(jnp.int32, (TILE, TILE), 0)
    column = lax.broadcasted_iota(jnp.int32, (TILE, TILE), 1)
    shared = row & column
    shared = shared ^ (shared >> 4)
    shared = shared ^ (shared >> 2)
    shared = shared ^ (shared >> 1)
    return (1 - 2 * (shared & 1)).astype(jnp.float32)


def flag_lines(offsets, devices, inner):
    count = offsets.shape[1]
    place = lax.broadcasted_iota(jnp.int32, (devices, count), 0)
    left = jnp.where(place == offsets // inner, 1.0, 0.0)
    lane = lax.broadcasted_iota(jnp.int32, (LANES, count), 0)
    right = jnp.where(lane == offsets % inner, 1.0, 0.0)
    return lax.dot_general(
        left.astype(jnp.bfloat16),
        right.astype(jnp.bfloat16),
        (((1,), (1,)), ((), ())),
        preferred_element_type=jnp.float32,
    )


def mix_kernel(devices, factor, signs_far, sampled_far, block, mixed, held, signs, sampled, arrive, small):
    groups, _, columns = block.shape
    inner = groups * TILE // devices
    lines = mixed.shape[0] // devices
    column_tiles = columns // LANES
    place = places(main_order(devices))
    quarter = groups // arrive.shape[0]
    signs_copy = pltpu.make_async_copy(signs_far, signs, small.at[0])
    sampled_copy = pltpu.make_async_copy(sampled_far, sampled, small.at[1])
    incoming = [
        pltpu.make_async_copy(block.at[pl.ds(start, quarter)], held.at[pl.ds(start, quarter)], arrive.at[number])
        for number, start in enumerate(range(0, groups, quarter))
    ]
    for copy in [signs_copy, sampled_copy] + incoming:
        copy.start()
    table = sign_table() * factor
    signs_copy.wait()
    flips = signs[...].astype(jnp.float32)
    due = {0: incoming[:1], quarter: incoming[1:-1], groups - quarter: incoming[-1:]}
    for g in range(groups):
        for copy in due.get(g, []):
            copy.wait()
        left = (table * flips[g : g + 1, :]).astype(jnp.bfloat16)
        high, middle, low = split3(held[g])
        held[g] = jnp.dot(left, low, preferred_element_type=jnp.float32) + jnp.dot(
            jnp.concatenate([left, left], axis=1),
            jnp.concatenate([middle, high], axis=0),
            preferred_element_type=jnp.float32,
        )
    sampled_copy.wait()
    offsets = jnp.concatenate([sampled[i : i + 1, :] for i in range(sampled.shape[0])], axis=1)
    flags = flag_lines(offsets, devices, inner)
    for number in range(devices):
        mixed[pl.ds(place[number] * lines + lines - 1, 1), :] = flags[number : number + 1, :]
    for start in range(0, TILE, SUBLANES):
        for column in range(column_tiles):
            value = butterfly(held[:, pl.ds(start, SUBLANES), pl.ds(column * LANES, LANES)])
            tile = (start % inner) // SUBLANES * column_tiles + column
            for g in range(groups):
                first = place[(g * TILE + start) // inner] * lines + tile * SUBLANES
                mixed[pl.ds(first, SUBLANES), :] = value[g]


def local_mix(matrix, signs, sampled, devices, factor):
    rows, columns = matrix.shape
    groups = rows // TILE
    lines = rows // devices * columns // LANES + 1
    far = pl.BlockSpec(memory_space=pltpu.HBM)
    stay = lambda value: pltpu.with_memory_space_constraint(value, pltpu.HBM)
    return pl.pallas_call(
        lambda *refs: mix_kernel(devices, factor, *refs),
        out_shape=pltpu.VMEM((devices * lines, LANES), jnp.float32),
        in_specs=[far, far, far],
        out_specs=pl.BlockSpec(memory_space=pltpu.VMEM),
        scratch_shapes=[
            pltpu.VMEM((groups, TILE, columns), jnp.float32),
            pltpu.VMEM((rows // LANES, LANES), jnp.int32),
            pltpu.VMEM((sampled.shape[0] // LANES, LANES), jnp.int32),
            pltpu.SemaphoreType.DMA((4,)),
            pltpu.SemaphoreType.DMA((2,)),
        ],
        compiler_params=pltpu.CompilerParams(vmem_limit_bytes=VMEM_BYTES),
        cost_estimate=pl.CostEstimate(
            flops=6 * rows * TILE * columns, bytes_accessed=8 * rows * columns, transcendentals=0
        ),
        name="local_mix",
    )(
        stay(signs.reshape(-1, LANES)),
        stay(sampled.reshape(-1, LANES)),
        stay(matrix.reshape(groups, TILE, columns)),
    )


def gram_kernel(scale, devices, side, block, mine, other, chosen, work, parts):
    lines = block.shape[0] // devices
    columns = mine.shape[2]
    column_tiles = columns // LANES
    tiles = lines // SUBLANES // column_tiles
    near = SUBLANES
    far = devices // near
    place = places(main_order(devices))
    sublane = lax.broadcasted_iota(jnp.int32, (SUBLANES, LANES), 0)
    lane = lax.broadcasted_iota(jnp.int32, (SUBLANES, LANES), 1)
    spread = [
        jnp.broadcast_to(block[pl.ds(place[number] * lines + lines - 1, 1), :], (SUBLANES, LANES))
        for number in range(devices)
    ]
    ones = jnp.ones((LANES, LANES), jnp.bfloat16)
    for tile in range(tiles):
        own = lane == sublane + tile * SUBLANES
        flags = jnp.concatenate([jnp.where(own, value, 0.0) for value in spread]).astype(jnp.bfloat16)
        chosen[tile] = jnp.dot(flags, ones, preferred_element_type=jnp.float32).reshape(devices, SUBLANES, LANES)
    depth = devices * SUBLANES
    for tile in range(tiles):
        for column in range(column_tiles):
            number = tile * column_tiles + column
            lanes = pl.ds(column * LANES, LANES)
            slot = work.at[number % 2]
            for start in range(near):
                value = butterfly(
                    jnp.stack(
                        [
                            block[pl.ds(place[start + near * step] * lines + number * SUBLANES, SUBLANES), :]
                            for step in range(far)
                        ]
                    )
                )
                for step in range(far):
                    slot[start + near * step] = value[step]
            for step in range(far):
                group = pl.ds(near * step, near)
                value = jnp.where(chosen[tile, group] != 0.0, butterfly(slot[group]), 0.0)
                high, low = split2(value.reshape(near * SUBLANES, LANES))
                rows = pl.ds(tile * depth + near * SUBLANES * step, near * SUBLANES)
                parts[rows, lanes] = high
                parts[rows, pl.ds(columns + column * LANES, LANES)] = low
    half = columns // 2
    product = lambda left, right: lax.dot_general(
        left, right, (((0,), (0,)), ((), ())), preferred_element_type=jnp.float32
    )
    top = product(parts[:, :half], parts[...])
    bottom = product(parts[:, half:columns], parts[:, half:])
    high = [top[:, :half], top[:, half:columns], bottom[:, :half]]
    cross = [top[:, columns : columns + half], top[:, columns + half :], bottom[:, half:columns], bottom[:, columns:]]
    middle = high[1] + (cross[1] + cross[2].T)
    gram = scale * jnp.concatenate(
        [
            jnp.concatenate([high[0] + (cross[0] + cross[0].T), middle], axis=1),
            jnp.concatenate([middle.T, high[2] + (cross[3] + cross[3].T)], axis=1),
        ],
        axis=0,
    )
    first_side = side[0] == 0
    out_rows = mine.shape[1]
    for number, chip in enumerate(last_order(mine.shape[0])):
        starts = [(2 * chip + half) * out_rows for half in range(2)]
        zero, one = [gram[start : start + out_rows] for start in starts]
        mine[number] = jnp.where(first_side, zero, one)
        other[number] = jnp.where(first_side, one, zero)


def local_gram(block, side, devices, columns, scale):
    lines = block.shape[0] // devices
    tiles = lines * LANES // columns // SUBLANES
    half = jax.ShapeDtypeStruct((devices // 2, columns // devices, columns), jnp.float32)
    vmem = pl.BlockSpec(memory_space=pltpu.VMEM)
    return pl.pallas_call(
        lambda *refs: gram_kernel(scale, devices, *refs),
        out_shape=(half, half),
        in_specs=[pl.BlockSpec(memory_space=pltpu.SMEM), vmem],
        out_specs=(vmem, vmem),
        scratch_shapes=[
            pltpu.VMEM((tiles, devices, SUBLANES, LANES), jnp.float32),
            pltpu.VMEM((2, devices, SUBLANES, LANES), jnp.float32),
            pltpu.VMEM((tiles * devices * SUBLANES, 2 * columns), jnp.bfloat16),
        ],
        compiler_params=pltpu.CompilerParams(vmem_limit_bytes=VMEM_BYTES),
        cost_estimate=pl.CostEstimate(
            flops=4 * tiles * SUBLANES * devices * columns * columns,
            bytes_accessed=4 * devices * lines * LANES,
            transcendentals=0,
        ),
        name="local_gram",
    )(side.reshape(1), block)


def chip_at(x, y, z):
    return ((y % 2 * 4 + z) * 4 + x) * 2 + y // 2


def coordinates(chip):
    return chip // 2 % 4, chip % 2 * 2 + chip // 32, chip // 8 % 4


def turned(chip):
    return chip_at(*[(c + 2) % 4 for c in coordinates(chip)])


def main_order(devices):
    order = []
    for place in range(devices // 2):
        y = place // 32 * 2 + place % 2
        chip = chip_at(place // 2 % 4, y, place // 8 % 4)
        order += [2 * chip, 2 * turned(chip) + 1]
    return order


def last_order(chips):
    return [turned(chip) for chip in range(chips)]


def places(order):
    return {device: place for place, device in enumerate(order)}


def local(matrix, sign_flips, sampled_rows):
    rows, columns = matrix.shape
    devices = lax.axis_size(AXIS)
    chips = devices // 2
    samples = sampled_rows.shape[0] * devices
    factor = 1.0 / math.sqrt(rows * devices)
    scale = 1.0 / samples

    side = lax.axis_index(AXIS) % 2
    mixed = local_mix(matrix, sign_flips, sampled_rows, devices, factor)
    mixed, side = lax.optimization_barrier((mixed, side))
    lines = mixed.shape[0] // devices
    blocks = lax.all_to_all(
        mixed.reshape(devices, lines * LANES), AXIS, 0, 0, axis_index_groups=[main_order(devices)], tiled=True
    )
    mine, other = local_gram(blocks.reshape(devices * lines, LANES), side, devices, columns, scale)

    summed = mine + lax.ppermute(other, AXIS, [(i, i ^ 1) for i in range(devices)])
    sides = [[2 * chip + side for chip in last_order(chips)] for side in range(2)]
    pieces = lax.all_to_all(summed, AXIS, 0, 0, axis_index_groups=sides, tiled=True)
    return jnp.sum(pieces, axis=0)


def solution(mesh):
    flat = Mesh(mesh.devices.reshape(-1), (AXIS,))
    return jax.shard_map(
        local, mesh=flat, in_specs=(P(AXIS, None), P(AXIS), P(AXIS)), out_specs=P(AXIS, None), check_vma=False
    )
```

```python
import math

import jax
import jax.numpy as jnp
from jax import lax
from jax.experimental import pallas as pl
from jax.experimental.pallas import tpu as pltpu
from jax.sharding import Mesh, PartitionSpec as P

AXIS = "d"
TILE = 128
LANES = 128
SUBLANES = 8
VMEM_BYTES = 32 << 20


def butterfly(value):
    count = value.shape[0]
    if count == 1:
        return value
    half = count // 2
    first, second = value[:half], value[half:]
    return jnp.concatenate([butterfly(first + second), butterfly(first - second)])


def split2(value):
    high = value.astype(jnp.bfloat16)
    low = (value - high.astype(jnp.float32)).astype(jnp.bfloat16)
    return high, low


def split3(value):
    high = value.astype(jnp.bfloat16)
    rest = value - high.astype(jnp.float32)
    middle = rest.astype(jnp.bfloat16)
    low = (rest - middle.astype(jnp.float32)).astype(jnp.bfloat16)
    return high, middle, low


def sign_table():
    row = lax.broadcasted_iota(jnp.int32, (TILE, TILE), 0)
    column = lax.broadcasted_iota(jnp.int32, (TILE, TILE), 1)
    shared = row & column
    shared = shared ^ (shared >> 4)
    shared = shared ^ (shared >> 2)
    shared = shared ^ (shared >> 1)
    return (1 - 2 * (shared & 1)).astype(jnp.float32)


def flag_lines(offsets, devices, inner):
    count = offsets.shape[1]
    place = lax.broadcasted_iota(jnp.int32, (devices, count), 0)
    left = jnp.where(place == offsets // inner, 1.0, 0.0)
    lane = lax.broadcasted_iota(jnp.int32, (LANES, count), 0)
    right = jnp.where(lane == offsets % inner, 1.0, 0.0)
    return lax.dot_general(
        left.astype(jnp.bfloat16),
        right.astype(jnp.bfloat16),
        (((1,), (1,)), ((), ())),
        preferred_element_type=jnp.float32,
    )


def mix_kernel(devices, factor, signs_far, sampled_far, block, mixed, held, signs, sampled, arrive, small):
    groups, _, columns = block.shape
    inner = groups * TILE // devices
    lines = mixed.shape[0] // devices
    column_tiles = columns // LANES
    place = places(main_order(devices))
    quarter = groups // arrive.shape[0]
    signs_copy = pltpu.make_async_copy(signs_far, signs, small.at[0])
    sampled_copy = pltpu.make_async_copy(sampled_far, sampled, small.at[1])
    incoming = [
        pltpu.make_async_copy(block.at[pl.ds(start, quarter)], held.at[pl.ds(start, quarter)], arrive.at[number])
        for number, start in enumerate(range(0, groups, quarter))
    ]
    for copy in [signs_copy, sampled_copy] + incoming:
        copy.start()
    table = sign_table() * factor
    signs_copy.wait()
    flips = signs[...].astype(jnp.float32)
    due = {0: incoming[:1], quarter: incoming[1:-1], groups - quarter: incoming[-1:]}
    for g in range(groups):
        for copy in due.get(g, []):
            copy.wait()
        left = (table * flips[g : g + 1, :]).astype(jnp.bfloat16)
        high, middle, low = split3(held[g])
        held[g] = jnp.dot(left, low, preferred_element_type=jnp.float32) + jnp.dot(
            jnp.concatenate([left, left], axis=1),
            jnp.concatenate([middle, high], axis=0),
            preferred_element_type=jnp.float32,
        )
    sampled_copy.wait()
    offsets = jnp.concatenate([sampled[i : i + 1, :] for i in range(sampled.shape[0])], axis=1)
    flags = flag_lines(offsets, devices, inner)
    for number in range(devices):
        mixed[pl.ds(place[number] * lines + lines - 1, 1), :] = flags[number : number + 1, :]
    for start in range(0, TILE, SUBLANES):
        for column in range(column_tiles):
            value = butterfly(held[:, pl.ds(start, SUBLANES), pl.ds(column * LANES, LANES)])
            tile = (start % inner) // SUBLANES * column_tiles + column
            for g in range(groups):
                first = place[(g * TILE + start) // inner] * lines + tile * SUBLANES
                mixed[pl.ds(first, SUBLANES), :] = value[g]


def local_mix(matrix, signs, sampled, devices, factor):
    rows, columns = matrix.shape
    groups = rows // TILE
    lines = rows // devices * columns // LANES + 1
    far = pl.BlockSpec(memory_space=pltpu.HBM)
    stay = lambda value: pltpu.with_memory_space_constraint(value, pltpu.HBM)
    return pl.pallas_call(
        lambda *refs: mix_kernel(devices, factor, *refs),
        out_shape=pltpu.VMEM((devices * lines, LANES), jnp.float32),
        in_specs=[far, far, far],
        out_specs=pl.BlockSpec(memory_space=pltpu.VMEM),
        scratch_shapes=[
            pltpu.VMEM((groups, TILE, columns), jnp.float32),
            pltpu.VMEM((rows // LANES, LANES), jnp.int32),
            pltpu.VMEM((sampled.shape[0] // LANES, LANES), jnp.int32),
            pltpu.SemaphoreType.DMA((4,)),
            pltpu.SemaphoreType.DMA((2,)),
        ],
        compiler_params=pltpu.CompilerParams(vmem_limit_bytes=VMEM_BYTES),
        cost_estimate=pl.CostEstimate(
            flops=6 * rows * TILE * columns, bytes_accessed=8 * rows * columns, transcendentals=0
        ),
        name="local_mix",
    )(
        stay(signs.reshape(-1, LANES)),
        stay(sampled.reshape(-1, LANES)),
        stay(matrix.reshape(groups, TILE, columns)),
    )


def gram_kernel(scale, devices, side, block, mine, other, chosen, work, parts):
    lines = block.shape[0] // devices
    columns = mine.shape[2]
    column_tiles = columns // LANES
    tiles = lines // SUBLANES // column_tiles
    near = SUBLANES
    far = devices // near
    place = places(main_order(devices))
    sublane = lax.broadcasted_iota(jnp.int32, (SUBLANES, LANES), 0)
    lane = lax.broadcasted_iota(jnp.int32, (SUBLANES, LANES), 1)
    spread = [
        jnp.broadcast_to(block[pl.ds(place[number] * lines + lines - 1, 1), :], (SUBLANES, LANES))
        for number in range(devices)
    ]
    ones = jnp.ones((LANES, LANES), jnp.bfloat16)
    for tile in range(tiles):
        own = lane == sublane + tile * SUBLANES
        flags = jnp.concatenate([jnp.where(own, value, 0.0) for value in spread]).astype(jnp.bfloat16)
        chosen[tile] = jnp.dot(flags, ones, preferred_element_type=jnp.float32).reshape(devices, SUBLANES, LANES)
    depth = devices * SUBLANES
    for tile in range(tiles):
        for column in range(column_tiles):
            number = tile * column_tiles + column
            lanes = pl.ds(column * LANES, LANES)
            slot = work.at[number % 2]
            for start in range(near):
                value = butterfly(
                    jnp.stack(
                        [
                            block[pl.ds(place[start + near * step] * lines + number * SUBLANES, SUBLANES), :]
                            for step in range(far)
                        ]
                    )
                )
                for step in range(far):
                    slot[start + near * step] = value[step]
            for step in range(far):
                group = pl.ds(near * step, near)
                value = jnp.where(chosen[tile, group] != 0.0, butterfly(slot[group]), 0.0)
                high, low = split2(value.reshape(near * SUBLANES, LANES))
                rows = pl.ds(tile * depth + near * SUBLANES * step, near * SUBLANES)
                parts[rows, lanes] = high
                parts[rows, pl.ds(columns + column * LANES, LANES)] = low
    half = columns // 2
    product = lambda left, right: lax.dot_general(
        left, right, (((0,), (0,)), ((), ())), preferred_element_type=jnp.float32
    )
    top = product(parts[:, :half], parts[...])
    bottom = product(parts[:, half:columns], parts[:, half:])
    high = [top[:, :half], top[:, half:columns], bottom[:, :half]]
    cross = [top[:, columns : columns + half], top[:, columns + half :], bottom[:, half:columns], bottom[:, columns:]]
    middle = high[1] + (cross[1] + cross[2].T)
    gram = scale * jnp.concatenate(
        [
            jnp.concatenate([high[0] + (cross[0] + cross[0].T), middle], axis=1),
            jnp.concatenate([middle.T, high[2] + (cross[3] + cross[3].T)], axis=1),
        ],
        axis=0,
    )
    first_side = side[0] == 0
    out_rows = mine.shape[1]
    for number, chip in enumerate(last_order(mine.shape[0])):
        starts = [(2 * chip + half) * out_rows for half in range(2)]
        zero, one = [gram[start : start + out_rows] for start in starts]
        mine[number] = jnp.where(first_side, zero, one)
        other[number] = jnp.where(first_side, one, zero)


def local_gram(block, side, devices, columns, scale):
    lines = block.shape[0] // devices
    tiles = lines * LANES // columns // SUBLANES
    half = jax.ShapeDtypeStruct((devices // 2, columns // devices, columns), jnp.float32)
    vmem = pl.BlockSpec(memory_space=pltpu.VMEM)
    return pl.pallas_call(
        lambda *refs: gram_kernel(scale, devices, *refs),
        out_shape=(half, half),
        in_specs=[pl.BlockSpec(memory_space=pltpu.SMEM), vmem],
        out_specs=(vmem, vmem),
        scratch_shapes=[
            pltpu.VMEM((tiles, devices, SUBLANES, LANES), jnp.float32),
            pltpu.VMEM((2, devices, SUBLANES, LANES), jnp.float32),
            pltpu.VMEM((tiles * devices * SUBLANES, 2 * columns), jnp.bfloat16),
        ],
        compiler_params=pltpu.CompilerParams(vmem_limit_bytes=VMEM_BYTES),
        cost_estimate=pl.CostEstimate(
            flops=4 * tiles * SUBLANES * devices * columns * columns,
            bytes_accessed=4 * devices * lines * LANES,
            transcendentals=0,
        ),
        name="local_gram",
    )(side.reshape(1), block)


def chip_at(x, y, z):
    return ((y % 2 * 4 + z) * 4 + x) * 2 + y // 2


def coordinates(chip):
    return chip // 2 % 4, chip % 2 * 2 + chip // 32, chip // 8 % 4


def turned(chip):
    return chip_at(*[(c + 2) % 4 for c in coordinates(chip)])


def main_order(devices):
    return [device for chip in range(devices // 2) for device in (2 * chip, 2 * turned(chip) + 1)]


def last_order(chips):
    return [turned(chip_at(place % 4, place // 4 % 4, place // 16)) for place in range(chips)]


def places(order):
    return {device: place for place, device in enumerate(order)}


def local(matrix, sign_flips, sampled_rows):
    rows, columns = matrix.shape
    devices = lax.axis_size(AXIS)
    chips = devices // 2
    samples = sampled_rows.shape[0] * devices
    factor = 1.0 / math.sqrt(rows * devices)
    scale = 1.0 / samples

    side = lax.axis_index(AXIS) % 2
    mixed = local_mix(matrix, sign_flips, sampled_rows, devices, factor)
    mixed, side = lax.optimization_barrier((mixed, side))
    lines = mixed.shape[0] // devices
    blocks = lax.all_to_all(
        mixed.reshape(devices, lines * LANES), AXIS, 0, 0, axis_index_groups=[main_order(devices)], tiled=True
    )
    mine, other = local_gram(blocks.reshape(devices * lines, LANES), side, devices, columns, scale)

    summed = mine + lax.ppermute(other, AXIS, [(i, i ^ 1) for i in range(devices)])
    sides = [[2 * chip + side for chip in last_order(chips)] for side in range(2)]
    pieces = lax.all_to_all(summed, AXIS, 0, 0, axis_index_groups=sides, tiled=True)
    return jnp.sum(pieces, axis=0)


def solution(mesh):
    flat = Mesh(mesh.devices.reshape(-1), (AXIS,))
    return jax.shard_map(
        local, mesh=flat, in_specs=(P(AXIS, None), P(AXIS), P(AXIS)), out_specs=P(AXIS, None), check_vma=False
    )
```
